512 devices in a mesh: ia: 8 (over y), ja: 8 (over z_lo, x), al: 8 (over z_hi, core).
Axes of the slice: x: 4, y: 8, z: 8 (z_hi: 4, z_lo: 2; z = z_hi * 2 + z_lo), core: 2. Of those that a mesh axis runs over, the one named last changes fastest.
Arguments:
- inputs: bfloat16 [12288, 1024], P(('ia', 'ja'), 'al'), may hold values from -6 to 6
- out_grad: bfloat16 [12288, 1024], P(('ia', 'ja'), 'al'), may hold values from -6 to 6
- pre_act: bfloat16 [24576, 1024], P(('ja', 'ia'), 'al'), may hold values from -8 to 8
- w_up: bfloat16 [12288, 24576], P(('ia', 'al'), 'ja'), may hold values from -0.0390625 to 0.0390625
- w_down: bfloat16 [12288, 24576], P(('ia', 'al'), 'ja'), may hold values from -0.0546875 to 0.0546875
Outputs:
- input_grad: bfloat16 [12288, 1024], P(('ia', 'ja'), 'al')
- up_grad: bfloat16 [12288, 24576], P(('ia', 'al'), 'ja')
- down_grad: bfloat16 [12288, 24576], P(('ia', 'al'), 'ja')
The draws below stay inside these ranges and needn't reach their ends.
All inputs are finite; a program needn't handle non-finite values.
Results may differ from the reference program's by a relative error of at most 0.025.
Values may be sent and summed in bfloat16 or wider, within the bound.
A program may use at most 128 MiB of HBM per device.

```python
import math
import jax
import jax.numpy as jnp
from jax import lax

D = 12288
FFC = 24576
TOK_DEV = 128
TOKENS = 1024
N_IA = 8
N_JA = 8
N_AL = 8


def level_of(own_key, extent, split, smallest, top_value):
    factor_of, own = 1.0, jax.random.fold_in(own_key, 6)
    for dim, shards_of in split:
        draws = jnp.exp(jax.random.uniform(jax.random.fold_in(own, dim), (shards_of,), jnp.float32, smallest / len(split), top_value / len(split)))
        factor_of = factor_of * jnp.repeat(draws, extent[dim] // shards_of).reshape([-1 if axis == dim else 1 for axis in range(len(extent))])
    return factor_of


def centred(rng, extent, scale, limit, pieces=(), dtype=jnp.bfloat16):
    drawn = jax.random.normal(rng, extent, jnp.float32) * scale
    if len(pieces) > 0:
        drawn = level_of(rng, extent, pieces, -0.22, 0.18) * drawn
    return jnp.clip(drawn, min=-limit, max=limit).astype(dtype)


def setup_inputs(seed: int = 0) -> dict:
    keys = jax.random.split(jax.random.key(seed), 6)
    inputs = centred(keys[0], (D, TOKENS), 1.0, 6.0, ((0, 64), (1, 8)))
    out_grad = centred(keys[1], (D, TOKENS), 1.0, 6.0, ((0, 64), (1, 8)))
    pre_act = centred(keys[2], (FFC, TOKENS), 1.5, 8.0, ((0, 64), (1, 8)))
    w_up = centred(keys[3], (D, FFC), FFC ** -0.5, 0.0390625, ((0, 64), (1, 8)))
    w_down = centred(keys[4], (D, FFC), D ** -0.5, 0.0546875, ((0, 64), (1, 8)))
    return dict(inputs=inputs, out_grad=out_grad, pre_act=pre_act, w_up=w_up, w_down=w_down)


gelu_root = math.sqrt(2.0 / math.pi)
gelu_cubic = 0.044715

def gelu_parts(pre):
    value = pre.astype(jnp.float32)
    tangent = jnp.tanh(gelu_root * (value + gelu_cubic * value * value * value))
    active = 0.5 * value * (1.0 + tangent)
    slope = 0.5 * (1.0 + tangent) + 0.5 * value * (1.0 - tangent * tangent) * gelu_root * (1.0 + 3.0 * gelu_cubic * value * value)
    return (active, slope)

def rounded(value):
    return lax.optimization_barrier(value.astype(jnp.bfloat16)).astype(jnp.float32)

def reference(inputs, out_grad, pre_act, w_up, w_down):
    width_block = D // N_IA
    hidden_block = FFC // N_JA
    act_grad = jnp.zeros((FFC, TOKENS), jnp.float32)
    for block in range(N_IA):
        lower = block * width_block
        term = jnp.dot(w_down[lower:lower + width_block].T, out_grad[lower:lower + width_block], preferred_element_type=jnp.float32)
        act_grad = act_grad + rounded(term)
    active, slope = gelu_parts(pre_act)
    act_full = active.astype(jnp.bfloat16)
    hidden_grad = (act_grad * slope).astype(jnp.bfloat16)
    input_sum = jnp.zeros((D, TOKENS), jnp.float32)
    for block in range(N_JA):
        lower = block * hidden_block
        term = jnp.dot(w_up[:, lower:lower + hidden_block], hidden_grad[lower:lower + hidden_block], preferred_element_type=jnp.float32)
        input_sum = input_sum + rounded(term)
    grad_scale = float(TOKENS) ** (-0.5)
    up_sum = jnp.zeros((D, FFC), jnp.float32)
    down_sum = jnp.zeros((D, FFC), jnp.float32)
    for block in range(N_AL):
        lower = block * TOK_DEV
        up_term = jnp.dot(inputs[:, lower:lower + TOK_DEV], hidden_grad[:, lower:lower + TOK_DEV].T, preferred_element_type=jnp.float32)
        up_sum = up_sum + rounded(up_term * grad_scale)
        down_term = jnp.dot(out_grad[:, lower:lower + TOK_DEV], act_full[:, lower:lower + TOK_DEV].T, preferred_element_type=jnp.float32)
        down_sum = down_sum + rounded(down_term * grad_scale)
    return (input_sum.astype(jnp.bfloat16), up_sum.astype(jnp.bfloat16), down_sum.astype(jnp.bfloat16))
```

```python
import functools
import math

import jax
import jax.numpy as jnp
from jax import lax
from jax.experimental import pallas as pl
from jax.experimental.pallas import tpu as pltpu
from jax.sharding import PartitionSpec as P

MESH = pl.DeviceIdType.MESH
BF16, F32 = jnp.bfloat16, jnp.float32
gelu_root = math.sqrt(2.0 / math.pi)
gelu_cubic = 0.044715

N = 8
Z = 4
TB = 128
FB = 384
M = 4
DB = 192
DC = 2 * DB
TH = Z * TB
RIGHT_HOPS = (4, 4, 3, 3)
Z_ORDER = (2, 1, 3, 0)


def gelu_parts(value):
    tangent = jnp.tanh(gelu_root * (value + gelu_cubic * value * value * value))
    active = 0.5 * value * (1.0 + tangent)
    slope = 0.5 * (1.0 + tangent) + 0.5 * value * (1.0 - tangent * tangent) * gelu_root * (
        1.0 + 3.0 * gelu_cubic * value * value
    )
    return active, slope


def hops(side, d):
    return RIGHT_HOPS[d] if side == 0 else N - 1 - RIGHT_HOPS[d]


def kernel(
    scale, x_ref, g_ref, pre_ref, wu_ref, wd_ref, ig_ref, du_ref, dd_ref,
    gbuf, xbuf, gt, wd_v, wu_v, p, rs, zrec, act, hg, pre_v, slope, part,
    stage_d, stage_u, qb, qt, qrec,
    loc_sem, pre_sem, g_ss, g_rs, x_ss, x_rs, tw_ss, tw_rs, w_ss, w_rs,
    a_zs, a_zr, a_ys, a_yr, r_zs, r_zr, r_ys, r_yr, h_zs, h_zr, h_ys, h_yr,
    o_ss, o_rs, q_ss, q_rs,
):
    i, j, a = lax.axis_index("ia"), lax.axis_index("ja"), lax.axis_index("al")
    zh, c = a // 2, a % 2
    par = i % 2
    own_rows = pl.ds(pl.multiple_of(c * DB, 64), DB)
    other_rows = pl.ds(pl.multiple_of((1 - c) * DB, 64), DB)
    twin = (i, j, a + 1 - 2 * c)
    y_to = ((lax.rem(i + 1, N), j, a), (lax.rem(i + N - 1, N), j, a))
    z_to = [(i, j, lax.rem(zh + d, Z) * 2 + c) for d in range(Z)]
    z_of = [lax.rem(zh + d, Z) for d in range(Z)]
    zsrc = [lax.rem(zh + Z - d, Z) for d in range(Z)]
    partner = (2 * (i // 2) + c, j, 2 * zh + par)
    spread = [(i, lax.rem(j + d, N), 2 * (j // 2) + c) for d in range(N)]
    collect = [(i, 2 * zh + e, 2 * zs + c) for e in range(2) for zs in range(Z)]
    home = j // 2 == zh
    pending = []

    def remote(src, dst, ss, rr, dev):
        return pltpu.make_async_remote_copy(
            src_ref=src, dst_ref=dst, send_sem=ss, recv_sem=rr, device_id=dev, device_id_type=MESH
        )

    def send(src, dst, ss, rr, dev):
        copy = remote(src, dst, ss, rr, dev)
        copy.start()
        pending.append(copy)

    def arrived(dst, ss, rr):
        remote(dst, dst, ss, rr, twin).wait_recv()

    def blk(buf, r, z):
        r = lax.rem(r + 2 * N, N)
        row = pl.multiple_of((r % 2) * TH + z * TB, TB)
        return buf.at[r // 2, pl.ds(row, TB), :]

    local = []
    for w_ref, w_v, s in ((wd_ref, wd_v, 0), (wu_ref, wu_v, 1)):
        for m in range(M):
            cols = pl.ds(pl.multiple_of((2 * m + c) * FB, 128), FB)
            cp = pltpu.make_async_copy(w_ref.at[:, cols], w_v.at[m, own_rows, :], loc_sem.at[s, m])
            cp.start()
            local.append(cp)

    barrier = pltpu.get_barrier_semaphore()

    def greet(dev):
        pl.semaphore_signal(barrier, inc=1, device_id=dev, device_id_type=MESH)

    for dev in (twin, y_to[0], y_to[1], z_to[1], z_to[2], z_to[3]):
        greet(dev)

    @pl.when(c != par)
    def _():
        greet(partner)

    for d in range(N):
        if d == 0:
            @pl.when(jnp.logical_not(home))
            def _():
                greet(spread[0])
        else:
            greet(spread[d])
    for dev in collect:
        @pl.when(jnp.logical_not((dev[1] == j) & (dev[2] == a)))
        def _():
            greet(dev)
    swap = jnp.where(c != par, 1, 0)
    both = jnp.where(home, 14, 16)
    pl.semaphore_wait(barrier, 6 + swap + both)

    def spread_start(src_ref, buf, ss, rr):
        row = pl.multiple_of((j % 2) * DB, 64)
        lane = pl.multiple_of(c * TH + zh * TB, TB)
        dst = buf.at[pl.ds(row, DB), pl.ds(lane, TB)]
        slot = (j % 2) * Z + zh

        @pl.when(home)
        def _():
            pltpu.make_async_copy(src_ref, dst, rr.at[slot]).start()

        @pl.when(jnp.logical_not(home))
        def _():
            remote(src_ref, dst, ss.at[0], rr.at[slot], spread[0]).start()

        for d in range(1, N):
            send(src_ref, dst, ss.at[d], rr.at[slot], spread[d])

    def spread_wait(src_ref, buf, ss, rr):
        for e in range(2):
            for zs in range(Z):
                lane = pl.multiple_of(c * TH + zs * TB, TB)
                arrived(buf.at[e * DB:(e + 1) * DB, pl.ds(lane, TB)], ss.at[0], rr.at[e * Z + zs])

    def spread_end(src_ref, buf, ss, rr):
        @pl.when(jnp.logical_not(home))
        def _():
            remote(src_ref, buf.at[0:DB, 0:TB], ss.at[0], rr.at[0], spread[0]).wait_send()

    own_half = pl.ds(pl.multiple_of(c * TH, TB), TH)
    other_half = pl.ds(pl.multiple_of((1 - c) * TH, TB), TH)

    spread_start(g_ref, gbuf, g_ss, g_rs)

    @pl.when(c == par)
    def _():
        pltpu.make_async_copy(pre_ref, pre_v, pre_sem.at[1]).start()

    @pl.when(c != par)
    def _():
        remote(pre_ref, pre_v, pre_sem.at[0], pre_sem.at[1], partner).start()

    def weights_to_twin(w_ref, w_v, s):
        for m in range(M):
            cols = pl.ds(pl.multiple_of((2 * m + 1 - c) * FB, 128), FB)
            send(w_ref.at[:, cols], w_v.at[m, own_rows, :], w_ss.at[s, m], w_rs.at[s, m], twin)

    def weights_wait(w_v, s):
        for m in range(M):
            local[s * M + m].wait()
            arrived(w_v.at[m, other_rows, :], w_ss.at[s, m], w_rs.at[s, m])

    weights_to_twin(wd_ref, wd_v, 0)

    arrived(pre_v, pre_sem.at[0], pre_sem.at[1])
    active, slope_now = gelu_parts(pre_v[...].astype(F32).T)
    blk(act, i, zh)[...] = active.astype(BF16)
    slope[...] = slope_now

    def ag_z(buf, zs, zr):
        for d in (2, 1, 3):
            send(blk(buf, i, zh), blk(buf, i, zh), zs.at[d], zr.at[d], z_to[d])

    def ag_z_wait(buf, zs, zr, d):
        arrived(blk(buf, i, zsrc[d]), zs.at[d], zr.at[d])

    def ag_send(buf, ys, yr, side, s, d):
        if s < hops(side, d):
            ref = blk(buf, i - s if side == 0 else i + s, zsrc[d])
            send(ref, ref, ys.at[side, s, d], yr.at[side, s, d], y_to[side])

    def ag_wait(buf, ys, yr, side, s, d):
        if s < hops(side, d):
            ref = blk(buf, i - s - 1 if side == 0 else i + s + 1, zsrc[d])
            arrived(ref, ys.at[side, s, d], yr.at[side, s, d])

    def ag_step(buf, ys, yr, s, ds=(0, 1, 3, 2)):
        for d in ds:
            for side in range(2):
                if s > 0:
                    ag_wait(buf, ys, yr, side, s - 1, d)
                ag_send(buf, ys, yr, side, s, d)

    ag_z(act, a_zs, a_zr)
    ag_step(act, a_ys, a_yr, 0, (0,))

    spread_wait(g_ref, gbuf, g_ss, g_rs)
    send(gbuf.at[:, own_half], gbuf.at[:, own_half], tw_ss.at[0], tw_rs.at[0], twin)

    def turn(tp):
        def one(z, carry):
            lane = pl.multiple_of(tp * TH + z * TB, TB)
            row = pl.multiple_of(z * TB, TB)
            gt[tp, pl.ds(row, TB), :] = gbuf[:, pl.ds(lane, TB)].T
            return carry
        lax.fori_loop(0, Z, one, 0)

    turn(c)
    spread_start(x_ref, xbuf, x_ss, x_rs)
    weights_to_twin(wu_ref, wu_v, 1)
    weights_wait(wd_v, 0)
    arrived(gbuf.at[:, other_half], tw_ss.at[0], tw_rs.at[0])
    turn(1 - c)

    def partial(r):
        r = lax.rem(r + 2 * N, N)
        row = pl.multiple_of((r % 2) * TH, TB)
        term = jnp.dot(gt[r % 2], wd_v[r // 2], preferred_element_type=F32)
        p[r // 2, pl.ds(row, TH), :] = term.astype(BF16)

    def rs_out(side, s, d):
        h = hops(side, d)
        return i + h - s if side == 0 else i - h + s

    def rs_send(side, s, d):
        src = blk(p, rs_out(side, s, d), z_of[d]) if s == 0 else rs.at[side, s - 1, d]
        send(src, rs.at[side, s, d], r_ys.at[side, s, d], r_yr.at[side, s, d], y_to[side])

    def rs_wait(side, s, d):
        arrived(rs.at[side, s, d], r_ys.at[side, s, d], r_yr.at[side, s, d])

    def rs_step(s):
        for d in Z_ORDER:
            for side in range(2):
                if s < hops(side, d) - 1:
                    rs_wait(side, s, d)
                    mine = blk(p, rs_out(side, s + 1, d), z_of[d])
                    got = rs.at[side, s, d]
                    got[...] = (got[...].astype(F32) + mine[...].astype(F32)).astype(BF16)
                    rs_send(side, s + 1, d)

    partial(i + 4)
    for d in Z_ORDER:
        rs_send(0 if hops(0, d) == 4 else 1, 0, d)
    partial(i + 3)
    partial(i - 3)
    for d in Z_ORDER:
        rs_send(1 if hops(0, d) == 4 else 0, 0, d)

    def rest(k, carry):
        partial(i + N - 2 + k)
        return carry
    lax.fori_loop(0, 5, rest, 0)

    ag_step(act, a_ys, a_yr, 1, (0,))
    for d in (1, 3, 2):
        ag_z_wait(act, a_zs, a_zr, d)
        ag_step(act, a_ys, a_yr, 0, (d,))
    rs_step(0)
    ag_step(act, a_ys, a_yr, 1, (1, 3, 2))
    spread_wait(x_ref, xbuf, x_ss, x_rs)
    send(xbuf.at[:, own_half], xbuf.at[:, own_half], tw_ss.at[1], tw_rs.at[1], twin)
    rs_step(1)
    ag_step(act, a_ys, a_yr, 2)
    rs_step(2)

    for d in Z_ORDER:
        total = blk(p, i, z_of[d])[...].astype(F32)
        for side in range(2):
            s = hops(side, d) - 1
            rs_wait(side, s, d)
            total = total + rs[side, s, d].astype(F32)
        if d == 0:
            part[...] = total
        else:
            out = rs.at[0, hops(0, d) - 1, d]
            out[...] = total.astype(BF16)
            send(out, zrec.at[d], r_zs.at[d], r_zr.at[d], z_to[d])
    ag_step(act, a_ys, a_yr, 3)
    total = part[...]
    for d in (1, 3, 2):
        arrived(zrec.at[d], r_zs.at[d], r_zr.at[d])
        total = total + zrec[d].astype(F32)
    blk(hg, i, zh)[...] = (total * slope[...]).astype(BF16)

    ag_z(hg, h_zs, h_zr)
    ag_step(hg, h_ys, h_yr, 0, (0,))

    def weight_grad(feat, hid, stage, m):
        term = jnp.dot(feat[...], hid[m], preferred_element_type=F32) * scale
        stage[m] = term.astype(BF16)

    outs = []

    def weight_out(stage, out_ref, s, m):
        cols = pl.ds(pl.multiple_of((2 * m + c) * FB, 128), FB)
        cp = pltpu.make_async_copy(stage.at[m, own_rows, :], out_ref.at[:, cols], loc_sem.at[2 + s, m])
        cp.start()
        outs.append(cp)
        send(stage.at[m, other_rows, :], out_ref.at[:, cols], o_ss.at[s, m], o_rs.at[s, m], twin)

    def weight_arrived(out_ref, s, m):
        cols = pl.ds(pl.multiple_of((2 * m + 1 - c) * FB, 128), FB)
        arrived(out_ref.at[:, cols], o_ss.at[s, m], o_rs.at[s, m])

    for d in range(Z):
        for side in range(2):
            ag_wait(act, a_ys, a_yr, side, 3, d)
    weight_grad(gbuf, act, stage_d, 0)
    weight_out(stage_d, dd_ref, 0, 0)
    ag_step(hg, h_ys, h_yr, 1, (0,))
    for d in (1, 3, 2):
        ag_z_wait(hg, h_zs, h_zr, d)
        ag_step(hg, h_ys, h_yr, 0, (d,))
    for m in (1, 2):
        weight_grad(gbuf, act, stage_d, m)
        weight_out(stage_d, dd_ref, 0, m)
    ag_step(hg, h_ys, h_yr, 2, (0,))
    ag_step(hg, h_ys, h_yr, 1, (1, 3, 2))
    weight_grad(gbuf, act, stage_d, 3)
    weight_out(stage_d, dd_ref, 0, 3)
    arrived(xbuf.at[:, other_half], tw_ss.at[1], tw_rs.at[1])
    weights_wait(wu_v, 1)
    ag_step(hg, h_ys, h_yr, 2, (1, 3, 2))
    ag_step(hg, h_ys, h_yr, 3)

    def input_part(tp):
        row = pl.multiple_of(tp * TH, TB)
        total = jnp.zeros((DC, TH), F32)
        for m in range(M):
            total = total + lax.dot_general(
                wu_v[m], hg[m, pl.ds(row, TH), :], (((1,), (1,)), ((), ())),
                preferred_element_type=F32,
            )
        qb[tp] = total.astype(BF16)

    early = 1 - par
    input_part(early)

    @pl.when(c != early)
    def _():
        remote(qb.at[early], qt, tw_ss.at[2], tw_rs.at[2], twin).start()

    for d in range(Z):
        for side in range(2):
            ag_wait(hg, h_ys, h_yr, side, 3, d)
    input_part(par)

    @pl.when(c != par)
    def _():
        remote(qb.at[par], qt, tw_ss.at[2], tw_rs.at[2], twin).start()

    weight_grad(xbuf, hg, stage_u, 0)
    weight_out(stage_u, du_ref, 1, 0)
    arrived(qt, tw_ss.at[2], tw_rs.at[2])
    qb[c] = (qb[c].astype(F32) + qt[...].astype(F32)).astype(BF16)
    for e in range(2):
        for zs in range(Z):
            dev = collect[e * Z + zs]
            mine = (dev[1] == j) & (dev[2] == a)
            src = qb.at[c, e * DB:(e + 1) * DB, zs * TB:(zs + 1) * TB]

            @pl.when(mine)
            def _():
                pltpu.make_async_copy(src, qrec.at[j], q_rs.at[j]).start()

            @pl.when(jnp.logical_not(mine))
            def _():
                remote(src, qrec.at[j], q_ss.at[e * Z + zs], q_rs.at[j], dev).start()

    for m in range(1, M):
        weight_grad(xbuf, hg, stage_u, m)
        weight_out(stage_u, du_ref, 1, m)

    total = jnp.zeros((DB, TB), F32)
    for d in range(N):
        arrived(qrec.at[d], q_ss.at[0], q_rs.at[d])
        total = total + qrec[d].astype(F32)
    ig_ref[...] = total.astype(BF16)

    for s, out_ref in ((0, dd_ref), (1, du_ref)):
        for m in range(M):
            weight_arrived(out_ref, s, m)
    for cp in outs:
        cp.wait()
    for copy in pending:
        copy.wait_send()
    spread_end(g_ref, gbuf, g_ss, g_rs)
    spread_end(x_ref, xbuf, x_ss, x_rs)

    @pl.when(c != par)
    def _():
        remote(pre_ref, pre_v, pre_sem.at[0], pre_sem.at[1], partner).wait_send()

    remote(qb.at[0], qt, tw_ss.at[2], tw_rs.at[2], twin).wait_send()
    for e in range(2):
        for zs in range(Z):
            dev = collect[e * Z + zs]
            src = qb.at[c, e * DB:(e + 1) * DB, zs * TB:(zs + 1) * TB]

            @pl.when(jnp.logical_not((dev[1] == j) & (dev[2] == a)))
            def _():
                remote(src, qrec.at[j], q_ss.at[e * Z + zs], q_rs.at[j], dev).wait_send()


def shards(inputs, out_grad, pre_act, w_up, w_down):
    scale = float(inputs.shape[1] * N) ** (-0.5)
    dma = pltpu.SemaphoreType.DMA
    any_spec = pl.BlockSpec(memory_space=pl.ANY)
    return pl.pallas_call(
        functools.partial(kernel, scale),
        out_shape=(
            jax.ShapeDtypeStruct((DB, TB), BF16),
            jax.ShapeDtypeStruct((DB, N * FB), BF16),
            jax.ShapeDtypeStruct((DB, N * FB), BF16),
        ),
        in_specs=[any_spec] * 5,
        out_specs=(pl.BlockSpec(memory_space=pltpu.VMEM), any_spec, any_spec),
        scratch_shapes=[
            pltpu.VMEM((DC, 2 * TH), BF16),
            pltpu.VMEM((DC, 2 * TH), BF16),
            pltpu.VMEM((2, TH, DC), BF16),
            pltpu.VMEM((M, DC, FB), BF16),
            pltpu.VMEM((M, DC, FB), BF16),
            pltpu.VMEM((M, 2 * TH, FB), BF16),
            pltpu.VMEM((2, 4, Z, TB, FB), BF16),
            pltpu.VMEM((Z, TB, FB), BF16),
            pltpu.VMEM((M, 2 * TH, FB), BF16),
            pltpu.VMEM((M, 2 * TH, FB), BF16),
            pltpu.VMEM((FB, TB), BF16),
            pltpu.VMEM((TB, FB), F32),
            pltpu.VMEM((TB, FB), F32),
            pltpu.VMEM((M, DC, FB), BF16),
            pltpu.VMEM((M, DC, FB), BF16),
            pltpu.VMEM((2, DC, TH), BF16),
            pltpu.VMEM((DC, TH), BF16),
            pltpu.VMEM((N, DB, TB), BF16),
            dma((4, M)), dma((2,)), dma((N,)), dma((N,)), dma((N,)), dma((N,)),
            dma((3,)), dma((3,)), dma((2, M)), dma((2, M)),
            dma((Z,)), dma((Z,)), dma((2, 4, Z)), dma((2, 4, Z)),
            dma((Z,)), dma((Z,)), dma((2, 4, Z)), dma((2, 4, Z)),
            dma((Z,)), dma((Z,)), dma((2, 4, Z)), dma((2, 4, Z)),
            dma((2, M)), dma((2, M)), dma((N,)), dma((N,)),
        ],
        compiler_params=pltpu.CompilerParams(
            collective_id=0, has_side_effects=True, vmem_limit_bytes=44 * 2**20
        ),
    )(inputs, out_grad, pre_act, w_up, w_down)


def solution(mesh):
    in_specs = (
        P(("ia", "ja"), "al"),
        P(("ia", "ja"), "al"),
        P(("ja", "ia"), "al"),
        P(("ia", "al"), "ja"),
        P(("ia", "al"), "ja"),
    )
    out_specs = (P(("ia", "ja"), "al"), P(("ia", "al"), "ja"), P(("ia", "al"), "ja"))
    return jax.shard_map(shards, mesh=mesh, in_specs=in_specs, out_specs=out_specs, check_vma=False)
```

```python
import functools
import math

import jax
import jax.numpy as jnp
from jax import lax
from jax.experimental import pallas as pl
from jax.experimental.pallas import tpu as pltpu
from jax.sharding import PartitionSpec as P

MESH = pl.DeviceIdType.MESH
BF16, F32 = jnp.bfloat16, jnp.float32
gelu_root = math.sqrt(2.0 / math.pi)
gelu_cubic = 0.044715

N = 8
Z = 4
TB = 128
FB = 384
M = 4
DB = 192
DC = 2 * DB
TH = Z * TB
RIGHT_HOPS = (4, 4, 3, 3)
Z_ORDER = (2, 1, 3, 0)
ACT_ROWS = 96
HB = TB // 2


def gelu_parts(value):
    tangent = jnp.tanh(gelu_root * (value + gelu_cubic * value * value * value))
    active = 0.5 * value * (1.0 + tangent)
    slope = 0.5 * (1.0 + tangent) + 0.5 * value * (1.0 - tangent * tangent) * gelu_root * (
        1.0 + 3.0 * gelu_cubic * value * value
    )
    return active, slope


def hops(side, d):
    return RIGHT_HOPS[d] if side == 0 else N - 1 - RIGHT_HOPS[d]


def kernel(
    scale, x_ref, g_ref, pre_ref, wu_ref, wd_ref, ig_ref, du_ref, dd_ref,
    gbuf, xbuf, gt, wd_v, wu_v, p, rs, zrec, act, hg, pre_v, slope, part,
    stage_d, stage_u, qb, qt, qrec, pre_own, act_own, qacc,
    loc_sem, pre_sem, act_sem, a_bs, a_br, g_ss, g_rs, x_ss, x_rs, tw_ss, tw_rs, w_ss, w_rs,
    a_zs, a_zr, a_ys, a_yr, r_zs, r_zr, r_ys, r_yr, h_zs, h_zr, h_ys, h_yr,
    o_ss, o_rs, q_ss, q_rs,
):
    i, j, a = lax.axis_index("ia"), lax.axis_index("ja"), lax.axis_index("al")
    zh, c = a // 2, a % 2
    par = i % 2
    own_rows = pl.ds(pl.multiple_of(c * DB, 64), DB)
    other_rows = pl.ds(pl.multiple_of((1 - c) * DB, 64), DB)
    twin = (i, j, a + 1 - 2 * c)
    y_to = ((lax.rem(i + 1, N), j, a), (lax.rem(i + N - 1, N), j, a))
    z_to = [(i, j, lax.rem(zh + d, Z) * 2 + c) for d in range(Z)]
    z_of = [lax.rem(zh + d, Z) for d in range(Z)]
    zsrc = [lax.rem(zh + Z - d, Z) for d in range(Z)]
    partner = (2 * (i // 2) + c, j, 2 * zh + par)
    spread = [(i, lax.rem(j + d, N), 2 * (j // 2) + c) for d in range(N)]
    collect = [(i, 2 * zh + e, 2 * zs + c) for e in range(2) for zs in range(Z)]
    home = j // 2 == zh
    pending = []

    def remote(src, dst, ss, rr, dev):
        return pltpu.make_async_remote_copy(
            src_ref=src, dst_ref=dst, send_sem=ss, recv_sem=rr, device_id=dev, device_id_type=MESH
        )

    def send(src, dst, ss, rr, dev):
        copy = remote(src, dst, ss, rr, dev)
        copy.start()
        pending.append(copy)

    def arrived(dst, ss, rr):
        remote(dst, dst, ss, rr, twin).wait_recv()

    def blk(buf, r, z, first=0, count=TB):
        r = lax.rem(r + 2 * N, N)
        row = pl.multiple_of((r % 2) * TH + z * TB + first, 16)
        return buf.at[r // 2, pl.ds(row, count), :]

    pre_in = pltpu.make_async_copy(pre_ref, pre_own, pre_sem.at[2])
    pre_in.start()

    local = []
    for w_ref, w_v, s in ((wd_ref, wd_v, 0), (wu_ref, wu_v, 1)):
        for m in range(M):
            cols = pl.ds(pl.multiple_of((2 * m + c) * FB, 128), FB)
            cp = pltpu.make_async_copy(w_ref.at[:, cols], w_v.at[m, own_rows, :], loc_sem.at[s, m])
            cp.start()
            local.append(cp)

    barrier = pltpu.get_barrier_semaphore()

    def greet(dev):
        pl.semaphore_signal(barrier, inc=1, device_id=dev, device_id_type=MESH)

    for dev in (twin, y_to[0], y_to[1], z_to[1], z_to[2], z_to[3]):
        greet(dev)

    @pl.when(c != par)
    def _():
        greet(partner)

    for d in range(N):
        if d == 0:
            @pl.when(jnp.logical_not(home))
            def _():
                greet(spread[0])
        else:
            greet(spread[d])
    for dev in collect:
        @pl.when(jnp.logical_not((dev[1] == j) & (dev[2] == a)))
        def _():
            greet(dev)
    swap = jnp.where(c != par, 1, 0)
    both = jnp.where(home, 14, 16)

    pre_in.wait()
    act_own[...] = gelu_parts(pre_own[...].astype(F32).T)[0].astype(BF16)
    pl.semaphore_wait(barrier, 6 + swap + both)

    def spread_start(src_ref, buf, ss, rr):
        row = pl.multiple_of((j % 2) * DB, 64)
        lane = pl.multiple_of(c * TH + zh * TB, TB)
        dst = buf.at[pl.ds(row, DB), pl.ds(lane, TB)]
        slot = (j % 2) * Z + zh

        @pl.when(home)
        def _():
            pltpu.make_async_copy(src_ref, dst, rr.at[slot]).start()

        @pl.when(jnp.logical_not(home))
        def _():
            remote(src_ref, dst, ss.at[0], rr.at[slot], spread[0]).start()

        for d in range(1, N):
            send(src_ref, dst, ss.at[d], rr.at[slot], spread[d])

    def spread_wait(src_ref, buf, ss, rr):
        for e in range(2):
            for zs in range(Z):
                lane = pl.multiple_of(c * TH + zs * TB, TB)
                arrived(buf.at[e * DB:(e + 1) * DB, pl.ds(lane, TB)], ss.at[0], rr.at[e * Z + zs])

    def spread_end(src_ref, buf, ss, rr):
        @pl.when(jnp.logical_not(home))
        def _():
            remote(src_ref, buf.at[0:DB, 0:TB], ss.at[0], rr.at[0], spread[0]).wait_send()

    own_half = pl.ds(pl.multiple_of(c * TH, TB), TH)
    other_half = pl.ds(pl.multiple_of((1 - c) * TH, TB), TH)

    spread_start(g_ref, gbuf, g_ss, g_rs)

    there = 2 * (i // 2) + c

    @pl.when(c == par)
    def _():
        pltpu.make_async_copy(act_own, blk(act, i, zh), act_sem.at[1]).start()
        pltpu.make_async_copy(pre_own, pre_v, pre_sem.at[1]).start()

    @pl.when(c != par)
    def _():
        remote(act_own, blk(act, there, zh), act_sem.at[0], act_sem.at[1], partner).start()
        remote(pre_own, pre_v, pre_sem.at[0], pre_sem.at[1], partner).start()

    def weights_to_twin(w_ref, w_v, s):
        for m in range(M):
            cols = pl.ds(pl.multiple_of((2 * m + 1 - c) * FB, 128), FB)
            send(w_ref.at[:, cols], w_v.at[m, own_rows, :], w_ss.at[s, m], w_rs.at[s, m], twin)

    def weights_wait(w_v, s):
        for m in range(M):
            local[s * M + m].wait()
            arrived(w_v.at[m, other_rows, :], w_ss.at[s, m], w_rs.at[s, m])

    weights_to_twin(wd_ref, wd_v, 0)

    class Gather:
        def __init__(self, buf, base, count, rows, sems):
            self.buf, self.base, self.count, self.rows, self.sems = buf, base, count, rows, sems

        def whole(self, r, z):
            return blk(self.buf, r, z, self.base, self.count)

        def first(self, r, z):
            return blk(self.buf, r, z, self.base, self.rows)

        def rest(self, r, z):
            return blk(self.buf, r, z, self.base + self.rows, self.count - self.rows)

        def z_start(self):
            zs, zr = self.sems[:2]
            for d in (2, 1, 3):
                ref = self.whole(i, zh)
                send(ref, ref, zs.at[d], zr.at[d], z_to[d])

        def z_wait(self, d):
            zs, zr = self.sems[:2]
            arrived(self.whole(i, zsrc[d]), zs.at[d], zr.at[d])

        def y_ref(self, r, d):
            return self.first(r, zsrc[d]) if d else self.whole(r, zh)

        def y_send(self, side, s, d):
            ys, yr = self.sems[2:4]
            if s < hops(side, d):
                ref = self.y_ref(i - s if side == 0 else i + s, d)
                send(ref, ref, ys.at[side, s, d], yr.at[side, s, d], y_to[side])

        def y_wait(self, side, s, d):
            ys, yr = self.sems[2:4]
            if s < hops(side, d):
                ref = self.y_ref(i - s - 1 if side == 0 else i + s + 1, d)
                arrived(ref, ys.at[side, s, d], yr.at[side, s, d])

        def b_send(self, side, s):
            if s < hops(side, 0) and self.rows < self.count:
                bs, br = self.sems[4:]
                ref = self.rest(i - s - 1 if side == 0 else i + s + 1, zh)
                for d in (2, 1, 3):
                    send(ref, ref, bs.at[side, s, d], br.at[side, s, d], z_to[d])

        def b_wait(self, s):
            for side in range(2):
                if s < hops(side, 0) and self.rows < self.count:
                    bs, br = self.sems[4:]
                    for d in (1, 3, 2):
                        ref = self.rest(i - s - 1 if side == 0 else i + s + 1, zsrc[d])
                        arrived(ref, bs.at[side, s, d], br.at[side, s, d])

        def step(self, s, ds):
            for d in ds:
                for side in range(2):
                    if s > 0:
                        self.y_wait(side, s - 1, d)
                    self.y_send(side, s, d)
                    if s > 0 and d == 0:
                        self.b_send(side, s - 1)

    far = (1, 3, 2)
    g_act = Gather(act, 0, TB, ACT_ROWS, (a_zs, a_zr, a_ys, a_yr, a_bs, a_br))
    g_hid = [
        Gather(hg, h * HB, HB, HB, (h_zs.at[h], h_zr.at[h], h_ys.at[h], h_yr.at[h])) for h in range(2)
    ]

    arrived(blk(act, i, zh), act_sem.at[0], act_sem.at[1])
    g_act.step(0, (0,))
    arrived(pre_v, pre_sem.at[0], pre_sem.at[1])
    slope[...] = gelu_parts(pre_v[...].astype(F32).T)[1]
    g_act.step(1, (0,))

    spread_wait(g_ref, gbuf, g_ss, g_rs)
    send(gbuf.at[:, own_half], gbuf.at[:, own_half], tw_ss.at[0], tw_rs.at[0], twin)

    def turn(tp):
        def one(z, carry):
            lane = pl.multiple_of(tp * TH + z * TB, TB)
            row = pl.multiple_of(z * TB, TB)
            gt[tp, pl.ds(row, TB), :] = gbuf[:, pl.ds(lane, TB)].T
            return carry
        lax.fori_loop(0, Z, one, 0)

    turn(c)
    weights_wait(wd_v, 0)
    arrived(gbuf.at[:, other_half], tw_ss.at[0], tw_rs.at[0])
    turn(1 - c)

    def partial(r):
        r = lax.rem(r + 2 * N, N)
        row = pl.multiple_of((r % 2) * TH, TB)
        term = jnp.dot(gt[r % 2], wd_v[r // 2], preferred_element_type=F32)
        p[r // 2, pl.ds(row, TH), :] = term.astype(BF16)

    def rs_out(side, s, d):
        h = hops(side, d)
        return i + h - s if side == 0 else i - h + s

    def rs_at(h, side, s, d):
        return rs.at[side, s, d, h * HB:(h + 1) * HB]

    def p_at(h, r, d):
        return blk(p, r, z_of[d], h * HB, HB)

    def rs_send(h, side, s, d):
        src = p_at(h, rs_out(side, s, d), d) if s == 0 else rs_at(h, side, s - 1, d)
        send(src, rs_at(h, side, s, d), r_ys.at[h, side, s, d], r_yr.at[h, side, s, d], y_to[side])

    def rs_wait(h, side, s, d):
        arrived(rs_at(h, side, s, d), r_ys.at[h, side, s, d], r_yr.at[h, side, s, d])

    def rs_start(h, long):
        for d in Z_ORDER:
            rs_send(h, 0 if (hops(0, d) == 4) == long else 1, 0, d)

    def rs_step(h, s):
        for d in Z_ORDER:
            for side in range(2):
                if s < hops(side, d) - 1:
                    rs_wait(h, side, s, d)
                    mine = p_at(h, rs_out(side, s + 1, d), d)
                    got = rs_at(h, side, s, d)
                    got[...] = (got[...].astype(F32) + mine[...].astype(F32)).astype(BF16)
                    rs_send(h, side, s + 1, d)

    def rs_end(h):
        for d in Z_ORDER:
            total = p_at(h, i, d)[...].astype(F32)
            for side in range(2):
                s = hops(side, d) - 1
                rs_wait(h, side, s, d)
                total = total + rs_at(h, side, s, d)[...].astype(F32)
            if d == 0:
                part[h * HB:(h + 1) * HB] = total
            else:
                out = rs_at(h, 0, hops(0, d) - 1, d)
                out[...] = total.astype(BF16)
                send(out, zrec.at[d, h * HB:(h + 1) * HB], r_zs.at[h, d], r_zr.at[h, d], z_to[d])

    def hidden(h):
        rows = slice(h * HB, (h + 1) * HB)
        total = part[rows]
        for d in far:
            arrived(zrec.at[d, rows], r_zs.at[h, d], r_zr.at[h, d])
            total = total + zrec[d, rows].astype(F32)
        blk(hg, i, zh, h * HB, HB)[...] = (total * slope[rows]).astype(BF16)
        g_hid[h].z_start()
        g_hid[h].step(0, (0,))

    def cross(gather):
        for d in far:
            gather.z_wait(d)
            gather.step(0, (d,))

    partial(i + 4)
    rs_start(0, True)
    partial(i + 3)
    partial(i - 3)
    rs_start(0, False)
    g_act.step(2, (0,))

    def rest(k, carry):
        partial(i + N - 2 + k)
        return carry
    lax.fori_loop(0, 5, rest, 0)

    g_act.z_start()
    rs_step(0, 0)
    rs_step(0, 1)
    g_act.step(3, (0,))
    rs_step(0, 2)
    rs_start(1, True)
    rs_start(1, False)
    weights_to_twin(wu_ref, wu_v, 1)
    g_act.step(4, (0,))
    rs_end(0)
    rs_step(1, 0)
    rs_step(1, 1)
    hidden(0)
    rs_step(1, 2)
    g_hid[0].step(1, (0,))
    cross(g_hid[0])
    rs_end(1)
    g_hid[0].step(2, (0,))
    g_hid[0].step(1, far)
    hidden(1)
    g_hid[0].step(3, (0,))
    g_hid[0].step(2, far)
    g_hid[1].step(1, (0,))
    cross(g_hid[1])
    spread_start(x_ref, xbuf, x_ss, x_rs)
    cross(g_act)
    g_hid[0].step(3, far)
    g_hid[1].step(2, (0,))
    g_hid[1].step(1, far)
    g_hid[0].step(4, (0,) + far)
    g_act.step(1, far)
    g_hid[1].step(3, (0,))
    g_hid[1].step(2, far)
    g_act.step(2, far)
    g_hid[1].step(3, far)
    spread_wait(x_ref, xbuf, x_ss, x_rs)
    send(xbuf.at[:, own_half], xbuf.at[:, own_half], tw_ss.at[1], tw_rs.at[1], twin)
    weights_wait(wu_v, 1)

    def weight_grad(feat, hid, stage, m):
        term = jnp.dot(feat[...], hid[m], preferred_element_type=F32) * scale
        stage[m] = term.astype(BF16)

    outs = []

    def weight_out(stage, out_ref, s, m):
        cols = pl.ds(pl.multiple_of((2 * m + c) * FB, 128), FB)
        cp = pltpu.make_async_copy(stage.at[m, own_rows, :], out_ref.at[:, cols], loc_sem.at[2 + s, m])
        cp.start()
        outs.append(cp)
        send(stage.at[m, other_rows, :], out_ref.at[:, cols], o_ss.at[s, m], o_rs.at[s, m], twin)

    def weight_arrived(out_ref, s, m):
        cols = pl.ds(pl.multiple_of((2 * m + 1 - c) * FB, 128), FB)
        arrived(out_ref.at[:, cols], o_ss.at[s, m], o_rs.at[s, m])

    early = 1 - par
    last = lax.rem(i + 4, N) // 2

    def input_part(tp, m):
        row = pl.multiple_of(tp * TH, TB)
        return lax.dot_general(
            wu_v[m], hg[m, pl.ds(row, TH), :], (((1,), (1,)), ((), ())),
            preferred_element_type=F32,
        )

    def input_to_twin(tp):
        @pl.when(c != tp)
        def _():
            remote(qb.at[tp], qt, tw_ss.at[2], tw_rs.at[2], twin).start()

    def input_out(tp):
        @pl.when(c == tp)
        def _():
            arrived(qt, tw_ss.at[2], tw_rs.at[2])
            qb[c] = (qb[c].astype(F32) + qt[...].astype(F32)).astype(BF16)
            for e in range(2):
                for zs in range(Z):
                    dev = collect[e * Z + zs]
                    mine = (dev[1] == j) & (dev[2] == a)
                    src = qb.at[c, e * DB:(e + 1) * DB, zs * TB:(zs + 1) * TB]

                    @pl.when(mine)
                    def _():
                        pltpu.make_async_copy(src, qrec.at[j], q_rs.at[j]).start()

                    @pl.when(jnp.logical_not(mine))
                    def _():
                        remote(src, qrec.at[j], q_ss.at[e * Z + zs], q_rs.at[j], dev).start()

    qacc[...] = input_part(early, 0)
    for m in range(1, M):
        qacc[...] += input_part(early, m)
    qb[early] = qacc[...].astype(BF16)
    input_to_twin(early)
    qacc[...] = input_part(par, lax.rem(last + 1, M))
    for m in (2, 3):
        qacc[...] += input_part(par, lax.rem(last + m, M))
    input_out(early)
    arrived(xbuf.at[:, other_half], tw_ss.at[1], tw_rs.at[1])
    for m in (1, 2, 3):
        weight_grad(xbuf, hg, stage_u, lax.rem(last + m, M))
        weight_out(stage_u, du_ref, 1, lax.rem(last + m, M))
    g_hid[1].step(4, (0,) + far)
    qb[par] = (qacc[...] + input_part(par, last)).astype(BF16)
    input_to_twin(par)
    g_act.step(3, far)
    weight_grad(xbuf, hg, stage_u, last)
    weight_out(stage_u, du_ref, 1, last)
    input_out(par)
    for step in range(4):
        g_act.b_wait(step)
    g_act.step(4, far)
    for m in range(M):
        weight_grad(gbuf, act, stage_d, m)
        weight_out(stage_d, dd_ref, 0, m)

    total = jnp.zeros((DB, TB), F32)
    for d in range(N):
        arrived(qrec.at[d], q_ss.at[0], q_rs.at[d])
        total = total + qrec[d].astype(F32)
    ig_ref[...] = total.astype(BF16)

    for s, out_ref in ((0, dd_ref), (1, du_ref)):
        for m in range(M):
            weight_arrived(out_ref, s, m)
    for cp in outs:
        cp.wait()
    for copy in pending:
        copy.wait_send()
    spread_end(g_ref, gbuf, g_ss, g_rs)
    spread_end(x_ref, xbuf, x_ss, x_rs)

    @pl.when(c != par)
    def _():
        remote(act_own, blk(act, there, zh), act_sem.at[0], act_sem.at[1], partner).wait_send()
        remote(pre_own, pre_v, pre_sem.at[0], pre_sem.at[1], partner).wait_send()

    remote(qb.at[0], qt, tw_ss.at[2], tw_rs.at[2], twin).wait_send()
    for e in range(2):
        for zs in range(Z):
            dev = collect[e * Z + zs]
            src = qb.at[c, e * DB:(e + 1) * DB, zs * TB:(zs + 1) * TB]

            @pl.when(jnp.logical_not((dev[1] == j) & (dev[2] == a)))
            def _():
                remote(src, qrec.at[j], q_ss.at[e * Z + zs], q_rs.at[j], dev).wait_send()


def shards(inputs, out_grad, pre_act, w_up, w_down):
    scale = float(inputs.shape[1] * N) ** (-0.5)
    dma = pltpu.SemaphoreType.DMA
    any_spec = pl.BlockSpec(memory_space=pl.ANY)
    return pl.pallas_call(
        functools.partial(kernel, scale),
        out_shape=(
            jax.ShapeDtypeStruct((DB, TB), BF16),
            jax.ShapeDtypeStruct((DB, N * FB), BF16),
            jax.ShapeDtypeStruct((DB, N * FB), BF16),
        ),
        in_specs=[any_spec] * 5,
        out_specs=(pl.BlockSpec(memory_space=pltpu.VMEM), any_spec, any_spec),
        scratch_shapes=[
            pltpu.VMEM((DC, 2 * TH), BF16),
            pltpu.VMEM((DC, 2 * TH), BF16),
            pltpu.VMEM((2, TH, DC), BF16),
            pltpu.VMEM((M, DC, FB), BF16),
            pltpu.VMEM((M, DC, FB), BF16),
            pltpu.VMEM((M, 2 * TH, FB), BF16),
            pltpu.VMEM((2, 4, Z, TB, FB), BF16),
            pltpu.VMEM((Z, TB, FB), BF16),
            pltpu.VMEM((M, 2 * TH, FB), BF16),
            pltpu.VMEM((M, 2 * TH, FB), BF16),
            pltpu.VMEM((FB, TB), BF16),
            pltpu.VMEM((TB, FB), F32),
            pltpu.VMEM((TB, FB), F32),
            pltpu.VMEM((M, DC, FB), BF16),
            pltpu.VMEM((M, DC, FB), BF16),
            pltpu.VMEM((2, DC, TH), BF16),
            pltpu.VMEM((DC, TH), BF16),
            pltpu.VMEM((N, DB, TB), BF16),
            pltpu.VMEM((FB, TB), BF16),
            pltpu.VMEM((TB, FB), BF16),
            pltpu.VMEM((DC, TH), F32),
            dma((4, M)), dma((3,)), dma((2,)), dma((2, 4, Z)), dma((2, 4, Z)),
             dma((N,)), dma((N,)), dma((N,)), dma((N,)),
            dma((3,)), dma((3,)), dma((2, M)), dma((2, M)),
            dma((Z,)), dma((Z,)), dma((2, 4, Z)), dma((2, 4, Z)),
            dma((2, Z)), dma((2, Z)), dma((2, 2, 4, Z)), dma((2, 2, 4, Z)),
            dma((2, Z)), dma((2, Z)), dma((2, 2, 4, Z)), dma((2, 2, 4, Z)),
            dma((2, M)), dma((2, M)), dma((N,)), dma((N,)),
        ],
        compiler_params=pltpu.CompilerParams(
            collective_id=0, has_side_effects=True, vmem_limit_bytes=60 * 2**20
        ),
    )(inputs, out_grad, pre_act, w_up, w_down)


def solution(mesh):
    in_specs = (
        P(("ia", "ja"), "al"),
        P(("ia", "ja"), "al"),
        P(("ja", "ia"), "al"),
        P(("ia", "al"), "ja"),
        P(("ia", "al"), "ja"),
    )
    out_specs = (P(("ia", "ja"), "al"), P(("ia", "al"), "ja"), P(("ia", "al"), "ja"))
    return jax.shard_map(shards, mesh=mesh, in_specs=in_specs, out_specs=out_specs, check_vma=False)
```

```python
import functools
import math

import jax
import jax.numpy as jnp
from jax import lax
from jax.experimental import pallas as pl
from jax.experimental.pallas import tpu as pltpu
from jax.sharding import PartitionSpec as P

MESH = pl.DeviceIdType.MESH
BF16, F32 = jnp.bfloat16, jnp.float32
gelu_root = math.sqrt(2.0 / math.pi)
gelu_cubic = 0.044715

N = 8
Z = 4
TB = 128
FB = 384
M = 4
DB = 192
DC = 2 * DB
TH = Z * TB
RIGHT_HOPS = (4, 4, 3, 3)
Z_ORDER = (2, 1, 3, 0)
ACT_ROWS = 96
HB = TB // 2


def gelu_parts(value):
    tangent = jnp.tanh(gelu_root * (value + gelu_cubic * value * value * value))
    active = 0.5 * value * (1.0 + tangent)
    slope = 0.5 * (1.0 + tangent) + 0.5 * value * (1.0 - tangent * tangent) * gelu_root * (
        1.0 + 3.0 * gelu_cubic * value * value
    )
    return active, slope


def hops(side, d):
    return RIGHT_HOPS[d] if side == 0 else N - 1 - RIGHT_HOPS[d]


def kernel(
    scale, x_ref, g_ref, pre_ref, wu_ref, wd_ref, ig_ref, du_ref, dd_ref,
    gbuf, xbuf, gt, wd_v, wu_v, p, rs, zrec, act, hg, pre_v, slope, part,
    stage_d, stage_u, qb, qt, qrec, pre_own, act_own, qacc,
    loc_sem, pre_sem, act_sem, a_bs, a_br, g_ss, g_rs, x_ss, x_rs, tw_ss, tw_rs, w_ss, w_rs,
    a_zs, a_zr, a_ys, a_yr, r_zs, r_zr, r_ys, r_yr, h_zs, h_zr, h_ys, h_yr,
    o_ss, o_rs, q_ss, q_rs,
):
    i, j, a = lax.axis_index("ia"), lax.axis_index("ja"), lax.axis_index("al")
    zh, c = a // 2, a % 2
    par = i % 2
    own_rows = pl.ds(pl.multiple_of(c * DB, 64), DB)
    other_rows = pl.ds(pl.multiple_of((1 - c) * DB, 64), DB)
    twin = (i, j, a + 1 - 2 * c)
    y_to = ((lax.rem(i + 1, N), j, a), (lax.rem(i + N - 1, N), j, a))
    z_to = [(i, j, lax.rem(zh + d, Z) * 2 + c) for d in range(Z)]
    z_of = [lax.rem(zh + d, Z) for d in range(Z)]
    zsrc = [lax.rem(zh + Z - d, Z) for d in range(Z)]
    partner = (2 * (i // 2) + c, j, 2 * zh + par)
    spread = [(i, lax.rem(j + d, N), 2 * (j // 2) + c) for d in range(N)]
    collect = [(i, 2 * zh + e, 2 * zs + c) for e in range(2) for zs in range(Z)]
    home = j // 2 == zh
    pending = []

    def remote(src, dst, ss, rr, dev):
        return pltpu.make_async_remote_copy(
            src_ref=src, dst_ref=dst, send_sem=ss, recv_sem=rr, device_id=dev, device_id_type=MESH
        )

    def send(src, dst, ss, rr, dev):
        copy = remote(src, dst, ss, rr, dev)
        copy.start()
        pending.append(copy)

    def arrived(dst, ss, rr):
        remote(dst, dst, ss, rr, twin).wait_recv()

    def blk(buf, r, z, first=0, count=TB):
        r = lax.rem(r + 2 * N, N)
        row = pl.multiple_of((r % 2) * TH + z * TB + first, 16)
        return buf.at[r // 2, pl.ds(row, count), :]

    pre_in = pltpu.make_async_copy(pre_ref, pre_own, pre_sem.at[2])
    pre_in.start()

    local = []
    for w_ref, w_v, s in ((wd_ref, wd_v, 0), (wu_ref, wu_v, 1)):
        for m in range(M):
            cols = pl.ds(pl.multiple_of((2 * m + c) * FB, 128), FB)
            cp = pltpu.make_async_copy(w_ref.at[:, cols], w_v.at[m, own_rows, :], loc_sem.at[s, m])
            cp.start()
            local.append(cp)

    barrier = pltpu.get_barrier_semaphore()

    def greet(dev):
        pl.semaphore_signal(barrier, inc=1, device_id=dev, device_id_type=MESH)

    for dev in (twin, y_to[0], y_to[1], z_to[1], z_to[2], z_to[3]):
        greet(dev)

    @pl.when(c != par)
    def _():
        greet(partner)

    for d in range(N):
        if d == 0:
            @pl.when(jnp.logical_not(home))
            def _():
                greet(spread[0])
        else:
            greet(spread[d])
    for dev in collect:
        @pl.when(jnp.logical_not((dev[1] == j) & (dev[2] == a)))
        def _():
            greet(dev)
    swap = jnp.where(c != par, 1, 0)
    both = jnp.where(home, 14, 16)

    pre_in.wait()
    act_own[...] = gelu_parts(pre_own[...].astype(F32).T)[0].astype(BF16)
    pl.semaphore_wait(barrier, 6 + swap + both)

    def spread_start(src_ref, buf, ss, rr):
        row = pl.multiple_of((j % 2) * DB, 64)
        lane = pl.multiple_of(c * TH + zh * TB, TB)
        dst = buf.at[pl.ds(row, DB), pl.ds(lane, TB)]
        slot = (j % 2) * Z + zh

        @pl.when(home)
        def _():
            pltpu.make_async_copy(src_ref, dst, rr.at[slot]).start()

        @pl.when(jnp.logical_not(home))
        def _():
            remote(src_ref, dst, ss.at[0], rr.at[slot], spread[0]).start()

        for d in range(1, N):
            send(src_ref, dst, ss.at[d], rr.at[slot], spread[d])

    def spread_wait(buf, ss, rr, zs):
        for e in range(2):
            lane = pl.multiple_of(c * TH + zs * TB, TB)
            arrived(buf.at[e * DB:(e + 1) * DB, pl.ds(lane, TB)], ss.at[0], rr.at[e * Z + zs])

    def to_twin(buf, s, zs):
        ref = buf.at[:, pl.ds(pl.multiple_of(c * TH + zs * TB, TB), TB)]
        send(ref, ref, tw_ss.at[s, zs], tw_rs.at[s, zs], twin)

    def from_twin(buf, s, zs):
        ref = buf.at[:, pl.ds(pl.multiple_of((1 - c) * TH + zs * TB, TB), TB)]
        arrived(ref, tw_ss.at[s, zs], tw_rs.at[s, zs])

    def spread_end(src_ref, buf, ss, rr):
        @pl.when(jnp.logical_not(home))
        def _():
            remote(src_ref, buf.at[0:DB, 0:TB], ss.at[0], rr.at[0], spread[0]).wait_send()

    spread_start(g_ref, gbuf, g_ss, g_rs)

    there = 2 * (i // 2) + c

    @pl.when(c == par)
    def _():
        pltpu.make_async_copy(act_own, blk(act, i, zh), act_sem.at[1]).start()
        pltpu.make_async_copy(pre_own, pre_v, pre_sem.at[1]).start()

    @pl.when(c != par)
    def _():
        remote(act_own, blk(act, there, zh), act_sem.at[0], act_sem.at[1], partner).start()
        remote(pre_own, pre_v, pre_sem.at[0], pre_sem.at[1], partner).start()

    def weights_to_twin(w_ref, w_v, s):
        for m in range(M):
            cols = pl.ds(pl.multiple_of((2 * m + 1 - c) * FB, 128), FB)
            send(w_ref.at[:, cols], w_v.at[m, own_rows, :], w_ss.at[s, m], w_rs.at[s, m], twin)

    def weights_wait(w_v, s):
        for m in range(M):
            local[s * M + m].wait()
            arrived(w_v.at[m, other_rows, :], w_ss.at[s, m], w_rs.at[s, m])

    weights_to_twin(wd_ref, wd_v, 0)

    class Gather:
        def __init__(self, buf, base, count, rows, sems):
            self.buf, self.base, self.count, self.rows, self.sems = buf, base, count, rows, sems

        def whole(self, r, z):
            return blk(self.buf, r, z, self.base, self.count)

        def first(self, r, z):
            return blk(self.buf, r, z, self.base, self.rows)

        def rest(self, r, z):
            return blk(self.buf, r, z, self.base + self.rows, self.count - self.rows)

        def z_start(self):
            zs, zr = self.sems[:2]
            for d in (2, 1, 3):
                ref = self.whole(i, zh)
                send(ref, ref, zs.at[d], zr.at[d], z_to[d])

        def z_wait(self, d):
            zs, zr = self.sems[:2]
            arrived(self.whole(i, zsrc[d]), zs.at[d], zr.at[d])

        def y_ref(self, r, d):
            return self.first(r, zsrc[d]) if d else self.whole(r, zh)

        def y_send(self, side, s, d):
            ys, yr = self.sems[2:4]
            if s < hops(side, d):
                ref = self.y_ref(i - s if side == 0 else i + s, d)
                send(ref, ref, ys.at[side, s, d], yr.at[side, s, d], y_to[side])

        def y_wait(self, side, s, d):
            ys, yr = self.sems[2:4]
            if s < hops(side, d):
                ref = self.y_ref(i - s - 1 if side == 0 else i + s + 1, d)
                arrived(ref, ys.at[side, s, d], yr.at[side, s, d])

        def b_send(self, side, s):
            if s < hops(side, 0) and self.rows < self.count:
                bs, br = self.sems[4:]
                ref = self.rest(i - s - 1 if side == 0 else i + s + 1, zh)
                for d in (2, 1, 3):
                    send(ref, ref, bs.at[side, s, d], br.at[side, s, d], z_to[d])

        def b_wait(self, s):
            for side in range(2):
                if s < hops(side, 0) and self.rows < self.count:
                    bs, br = self.sems[4:]
                    for d in (1, 3, 2):
                        ref = self.rest(i - s - 1 if side == 0 else i + s + 1, zsrc[d])
                        arrived(ref, bs.at[side, s, d], br.at[side, s, d])

        def step(self, s, ds):
            for d in ds:
                for side in range(2):
                    if s > 0:
                        self.y_wait(side, s - 1, d)
                    self.y_send(side, s, d)

        def low(self, steps):
            for s in steps:
                for side in range(2):
                    self.b_send(side, s)

    far = (1, 3, 2)
    g_act = Gather(act, 0, TB, ACT_ROWS, (a_zs, a_zr, a_ys, a_yr, a_bs, a_br))
    g_hid = [
        Gather(hg, h * HB, HB, HB, (h_zs.at[h], h_zr.at[h], h_ys.at[h], h_yr.at[h])) for h in range(2)
    ]

    arrived(blk(act, i, zh), act_sem.at[0], act_sem.at[1])
    g_act.step(0, (0,))
    arrived(pre_v, pre_sem.at[0], pre_sem.at[1])
    slope[...] = gelu_parts(pre_v[...].astype(F32).T)[1]
    g_act.step(1, (0,))

    def turn(tp, zs):
        lane = pl.multiple_of(tp * TH + zs * TB, TB)
        gt[tp, zs * TB:(zs + 1) * TB, :] = gbuf[:, pl.ds(lane, TB)].T

    for zs in range(Z):
        spread_wait(gbuf, g_ss, g_rs, zs)
        to_twin(gbuf, 0, zs)
        turn(c, zs)
    weights_wait(wd_v, 0)
    for zs in range(Z):
        from_twin(gbuf, 0, zs)
        turn(1 - c, zs)

    def partial(r):
        r = lax.rem(r + 2 * N, N)
        row = pl.multiple_of((r % 2) * TH, TB)
        term = jnp.dot(gt[r % 2], wd_v[r // 2], preferred_element_type=F32)
        p[r // 2, pl.ds(row, TH), :] = term.astype(BF16)

    def rs_out(side, s, d):
        h = hops(side, d)
        return i + h - s if side == 0 else i - h + s

    def rs_at(h, side, s, d):
        return rs.at[side, s, d, h * HB:(h + 1) * HB]

    def p_at(h, r, d):
        return blk(p, r, z_of[d], h * HB, HB)

    def rs_send(h, side, s, d):
        src = p_at(h, rs_out(side, s, d), d) if s == 0 else rs_at(h, side, s - 1, d)
        send(src, rs_at(h, side, s, d), r_ys.at[h, side, s, d], r_yr.at[h, side, s, d], y_to[side])

    def rs_wait(h, side, s, d):
        arrived(rs_at(h, side, s, d), r_ys.at[h, side, s, d], r_yr.at[h, side, s, d])

    def rs_start(h, long):
        for d in Z_ORDER:
            rs_send(h, 0 if (hops(0, d) == 4) == long else 1, 0, d)

    def rs_step(h, s):
        for d in Z_ORDER:
            for side in range(2):
                if s < hops(side, d) - 1:
                    rs_wait(h, side, s, d)
                    mine = p_at(h, rs_out(side, s + 1, d), d)
                    got = rs_at(h, side, s, d)
                    got[...] = (got[...].astype(F32) + mine[...].astype(F32)).astype(BF16)
                    rs_send(h, side, s + 1, d)

    def rs_end(h):
        for d in Z_ORDER:
            total = p_at(h, i, d)[...].astype(F32)
            for side in range(2):
                s = hops(side, d) - 1
                rs_wait(h, side, s, d)
                total = total + rs_at(h, side, s, d)[...].astype(F32)
            if d == 0:
                part[h * HB:(h + 1) * HB] = total
            else:
                out = rs_at(h, 0, hops(0, d) - 1, d)
                out[...] = total.astype(BF16)
                send(out, zrec.at[d, h * HB:(h + 1) * HB], r_zs.at[h, d], r_zr.at[h, d], z_to[d])

    def hidden(h):
        rows = slice(h * HB, (h + 1) * HB)
        total = part[rows]
        for d in far:
            arrived(zrec.at[d, rows], r_zs.at[h, d], r_zr.at[h, d])
            total = total + zrec[d, rows].astype(F32)
        blk(hg, i, zh, h * HB, HB)[...] = (total * slope[rows]).astype(BF16)
        g_hid[h].z_start()
        g_hid[h].step(0, (0,))

    def cross(gather):
        for d in far:
            gather.z_wait(d)
            gather.step(0, (d,))

    partial(i + 4)
    rs_start(0, True)
    partial(i + 3)
    partial(i - 3)
    rs_start(0, False)
    g_act.step(2, (0,))

    def rest(k, carry):
        partial(i + N - 2 + k)
        return carry
    lax.fori_loop(0, 5, rest, 0)

    g_act.z_start()
    rs_step(0, 0)
    rs_step(0, 1)
    g_act.low((0, 1))
    g_act.step(3, (0,))
    rs_step(0, 2)
    rs_start(1, True)
    rs_start(1, False)
    weights_to_twin(wu_ref, wu_v, 1)
    g_act.step(4, (0,))
    rs_end(0)
    rs_step(1, 0)
    rs_step(1, 1)
    hidden(0)
    rs_step(1, 2)
    g_hid[0].step(1, (0,))
    cross(g_hid[0])
    rs_end(1)
    g_hid[0].step(2, (0,))
    g_hid[0].step(1, far)
    hidden(1)
    g_hid[0].step(3, (0,))
    g_hid[0].step(2, far)
    g_hid[1].step(1, (0,))
    cross(g_hid[1])
    g_act.low((2, 3))
    spread_start(x_ref, xbuf, x_ss, x_rs)
    g_hid[0].step(3, far)
    g_hid[1].step(2, (0,))
    g_hid[1].step(1, far)
    cross(g_act)
    g_hid[0].step(4, (0,) + far)
    g_hid[1].step(3, (0,))
    g_hid[1].step(2, far)
    g_hid[1].step(3, far)
    g_act.step(1, far)
    weights_wait(wu_v, 1)

    def weight_grad(feat, hid, stage, m):
        term = jnp.dot(feat[...], hid[m], preferred_element_type=F32) * scale
        stage[m] = term.astype(BF16)

    outs = []

    def weight_out(stage, out_ref, s, m):
        cols = pl.ds(pl.multiple_of((2 * m + c) * FB, 128), FB)
        cp = pltpu.make_async_copy(stage.at[m, own_rows, :], out_ref.at[:, cols], loc_sem.at[2 + s, m])
        cp.start()
        outs.append(cp)
        send(stage.at[m, other_rows, :], out_ref.at[:, cols], o_ss.at[s, m], o_rs.at[s, m], twin)

    def weight_arrived(out_ref, s, m):
        cols = pl.ds(pl.multiple_of((2 * m + 1 - c) * FB, 128), FB)
        arrived(out_ref.at[:, cols], o_ss.at[s, m], o_rs.at[s, m])

    early = 1 - par
    last = lax.rem(i + 4, N) // 2

    def input_part(tp, m):
        row = pl.multiple_of(tp * TH, TB)
        return lax.dot_general(
            wu_v[m], hg[m, pl.ds(row, TH), :], (((1,), (1,)), ((), ())),
            preferred_element_type=F32,
        )

    def input_done(tp, zs, total):
        qb[tp, :, zs * TB:(zs + 1) * TB] = total.astype(BF16)

        @pl.when(c != tp)
        def _():
            cols = slice(zs * TB, (zs + 1) * TB)
            remote(qb.at[tp, :, cols], qt.at[:, cols], tw_ss.at[2, zs], tw_rs.at[2, zs], twin).start()

    def input_out(tp):
        @pl.when(c == tp)
        def _():
            for zs in range(Z):
                cols = slice(zs * TB, (zs + 1) * TB)
                arrived(qt.at[:, cols], tw_ss.at[2, zs], tw_rs.at[2, zs])
                qb[c, :, cols] = (qb[c, :, cols].astype(F32) + qt[:, cols].astype(F32)).astype(BF16)
                for e in range(2):
                    dev = collect[e * Z + zs]
                    mine = (dev[1] == j) & (dev[2] == a)
                    src = qb.at[c, e * DB:(e + 1) * DB, cols]

                    @pl.when(mine)
                    def _():
                        pltpu.make_async_copy(src, qrec.at[j], q_rs.at[j]).start()

                    @pl.when(jnp.logical_not(mine))
                    def _():
                        remote(src, qrec.at[j], q_ss.at[e * Z + zs], q_rs.at[j], dev).start()

    qacc[...] = input_part(early, 0)
    for m in range(1, M):
        qacc[...] += input_part(early, m)
    for zs in range(Z):
        input_done(early, zs, qacc[:, zs * TB:(zs + 1) * TB])
    qacc[...] = input_part(par, lax.rem(last + 1, M))
    for m in (2, 3):
        qacc[...] += input_part(par, lax.rem(last + m, M))
    input_out(early)
    for zs in range(Z):
        spread_wait(xbuf, x_ss, x_rs, zs)
        to_twin(xbuf, 1, zs)
    g_hid[1].step(4, (0,) + far)
    for zs in range(Z):
        row = pl.multiple_of(par * TH + zs * TB, TB)
        term = lax.dot_general(
            wu_v[last], hg[last, pl.ds(row, TB), :], (((1,), (1,)), ((), ())),
            preferred_element_type=F32,
        )
        input_done(par, zs, qacc[:, zs * TB:(zs + 1) * TB] + term)
    g_act.step(2, far)
    input_out(par)
    for zs in range(Z):
        from_twin(xbuf, 1, zs)
    for m in (1, 2, 3):
        weight_grad(xbuf, hg, stage_u, lax.rem(last + m, M))
        weight_out(stage_u, du_ref, 1, lax.rem(last + m, M))
    weight_grad(xbuf, hg, stage_u, last)
    weight_out(stage_u, du_ref, 1, last)
    g_act.step(3, far)
    for step in range(4):
        g_act.b_wait(step)
    for m in (1, 2, 3):
        weight_grad(gbuf, act, stage_d, lax.rem(last + m, M))
        weight_out(stage_d, dd_ref, 0, lax.rem(last + m, M))
    g_act.step(4, far)
    weight_grad(gbuf, act, stage_d, last)
    weight_out(stage_d, dd_ref, 0, last)

    total = jnp.zeros((DB, TB), F32)
    for d in range(N):
        arrived(qrec.at[d], q_ss.at[0], q_rs.at[d])
        total = total + qrec[d].astype(F32)
    ig_ref[...] = total.astype(BF16)

    for s, out_ref in ((0, dd_ref), (1, du_ref)):
        for m in range(M):
            weight_arrived(out_ref, s, m)
    for cp in outs:
        cp.wait()
    for copy in pending:
        copy.wait_send()
    spread_end(g_ref, gbuf, g_ss, g_rs)
    spread_end(x_ref, xbuf, x_ss, x_rs)

    @pl.when(c != par)
    def _():
        remote(act_own, blk(act, there, zh), act_sem.at[0], act_sem.at[1], partner).wait_send()
        remote(pre_own, pre_v, pre_sem.at[0], pre_sem.at[1], partner).wait_send()

    for zs in range(Z):
        cols = slice(zs * TB, (zs + 1) * TB)
        remote(qb.at[0, :, cols], qt.at[:, cols], tw_ss.at[2, zs], tw_rs.at[2, zs], twin).wait_send()
    for e in range(2):
        for zs in range(Z):
            dev = collect[e * Z + zs]
            src = qb.at[c, e * DB:(e + 1) * DB, zs * TB:(zs + 1) * TB]

            @pl.when(jnp.logical_not((dev[1] == j) & (dev[2] == a)))
            def _():
                remote(src, qrec.at[j], q_ss.at[e * Z + zs], q_rs.at[j], dev).wait_send()


def hand_over(ig_in, du_in, dd_in, ig_out, du_out, dd_out, ig_v, du_v, dd_v, in_sem, out_sem):
    parts = [(ig_in, ig_v, ig_out)]
    for src, mid, dst in ((du_in, du_v, du_out), (dd_in, dd_v, dd_out)):
        for part in range(4):
            rows = pl.ds(part * (DB // 4), DB // 4)
            parts.append((src.at[rows, :], mid.at[rows, :], dst.at[rows, :]))
    loads = [pltpu.make_async_copy(src, mid, in_sem.at[n]) for n, (src, mid, _) in enumerate(parts)]
    stores = [pltpu.make_async_copy(mid, dst, out_sem.at[n]) for n, (_, mid, dst) in enumerate(parts)]
    for load in loads:
        load.start()
    for load, store in zip(loads, stores):
        load.wait()
        store.start()
    for store in stores:
        store.wait()


def shards(inputs, out_grad, pre_act, w_up, w_down):
    scale = float(inputs.shape[1] * N) ** (-0.5)
    dma = pltpu.SemaphoreType.DMA
    any_spec = pl.BlockSpec(memory_space=pl.ANY)
    results = pl.pallas_call(
        functools.partial(kernel, scale),
        out_shape=(
            jax.ShapeDtypeStruct((DB, TB), BF16),
            jax.ShapeDtypeStruct((DB, N * FB), BF16),
            jax.ShapeDtypeStruct((DB, N * FB), BF16),
        ),
        in_specs=[any_spec] * 5,
        out_specs=(pl.BlockSpec(memory_space=pltpu.VMEM), any_spec, any_spec),
        scratch_shapes=[
            pltpu.VMEM((DC, 2 * TH), BF16),
            pltpu.VMEM((DC, 2 * TH), BF16),
            pltpu.VMEM((2, TH, DC), BF16),
            pltpu.VMEM((M, DC, FB), BF16),
            pltpu.VMEM((M, DC, FB), BF16),
            pltpu.VMEM((M, 2 * TH, FB), BF16),
            pltpu.VMEM((2, 4, Z, TB, FB), BF16),
            pltpu.VMEM((Z, TB, FB), BF16),
            pltpu.VMEM((M, 2 * TH, FB), BF16),
            pltpu.VMEM((M, 2 * TH, FB), BF16),
            pltpu.VMEM((FB, TB), BF16),
            pltpu.VMEM((TB, FB), F32),
            pltpu.VMEM((TB, FB), F32),
            pltpu.VMEM((M, DC, FB), BF16),
            pltpu.VMEM((M, DC, FB), BF16),
            pltpu.VMEM((2, DC, TH), BF16),
            pltpu.VMEM((DC, TH), BF16),
            pltpu.VMEM((N, DB, TB), BF16),
            pltpu.VMEM((FB, TB), BF16),
            pltpu.VMEM((TB, FB), BF16),
            pltpu.VMEM((DC, TH), F32),
            dma((4, M)), dma((3,)), dma((2,)), dma((2, 4, Z)), dma((2, 4, Z)),
             dma((N,)), dma((N,)), dma((N,)), dma((N,)),
            dma((3, Z)), dma((3, Z)), dma((2, M)), dma((2, M)),
            dma((Z,)), dma((Z,)), dma((2, 4, Z)), dma((2, 4, Z)),
            dma((2, Z)), dma((2, Z)), dma((2, 2, 4, Z)), dma((2, 2, 4, Z)),
            dma((2, Z)), dma((2, Z)), dma((2, 2, 4, Z)), dma((2, 2, 4, Z)),
            dma((2, M)), dma((2, M)), dma((N,)), dma((N,)),
        ],
        compiler_params=pltpu.CompilerParams(
            collective_id=0, has_side_effects=True, vmem_limit_bytes=60 * 2**20
        ),
    )(inputs, out_grad, pre_act, w_up, w_down)
    return pl.pallas_call(
        hand_over,
        out_shape=[jax.ShapeDtypeStruct(value.shape, value.dtype) for value in results],
        in_specs=[any_spec] * 3,
        out_specs=[any_spec] * 3,
        scratch_shapes=[pltpu.VMEM(value.shape, value.dtype) for value in results] + [dma((9,)), dma((9,))],
        compiler_params=pltpu.CompilerParams(vmem_limit_bytes=60 * 2**20),
    )(*results)


def solution(mesh):
    in_specs = (
        P(("ia", "ja"), "al"),
        P(("ia", "ja"), "al"),
        P(("ja", "ia"), "al"),
        P(("ia", "al"), "ja"),
        P(("ia", "al"), "ja"),
    )
    out_specs = (P(("ia", "ja"), "al"), P(("ia", "al"), "ja"), P(("ia", "al"), "ja"))
    return jax.shard_map(shards, mesh=mesh, in_specs=in_specs, out_specs=out_specs, check_vma=False)
```

```python
import functools
import math

import jax
import jax.numpy as jnp
from jax import lax
from jax.experimental import pallas as pl
from jax.experimental.pallas import tpu as pltpu
from jax.sharding import PartitionSpec as P

MESH = pl.DeviceIdType.MESH
BF16, F32 = jnp.bfloat16, jnp.float32
gelu_root = math.sqrt(2.0 / math.pi)
gelu_cubic = 0.044715

N = 8
Z = 4
TB = 128
FB = 384
M = 4
DB = 192
DC = 2 * DB
TH = Z * TB
RIGHT_HOPS = (4, 4, 3, 3)
Z_ORDER = (2, 1, 3, 0)
ACT_ROWS = 96
HB = TB // 2


def gelu_parts(value):
    tangent = jnp.tanh(gelu_root * (value + gelu_cubic * value * value * value))
    active = 0.5 * value * (1.0 + tangent)
    slope = 0.5 * (1.0 + tangent) + 0.5 * value * (1.0 - tangent * tangent) * gelu_root * (
        1.0 + 3.0 * gelu_cubic * value * value
    )
    return active, slope


def hops(side, d):
    return RIGHT_HOPS[d] if side == 0 else N - 1 - RIGHT_HOPS[d]


def kernel(
    scale, x_ref, g_ref, pre_ref, wu_ref, wd_ref, ig_ref, du_ref, dd_ref,
    gbuf, xbuf, gt, wd_v, wu_v, p, rs, zrec, act, hg, pre_v, slope, part,
    stage_d, stage_u, qb, qt, qrec, pre_own, act_own, qacc,
    loc_sem, pre_sem, act_sem, a_bs, a_br, g_ss, g_rs, x_ss, x_rs, tw_ss, tw_rs, w_ss, w_rs,
    a_zs, a_zr, a_ys, a_yr, r_zs, r_zr, r_ys, r_yr, h_zs, h_zr, h_ys, h_yr,
    o_ss, o_rs, q_ss, q_rs,
):
    i, j, a = lax.axis_index("ia"), lax.axis_index("ja"), lax.axis_index("al")
    zh, c = a // 2, a % 2
    par = i % 2
    own_rows = pl.ds(pl.multiple_of(c * DB, 64), DB)
    other_rows = pl.ds(pl.multiple_of((1 - c) * DB, 64), DB)
    twin = (i, j, a + 1 - 2 * c)
    y_to = ((lax.rem(i + 1, N), j, a), (lax.rem(i + N - 1, N), j, a))
    z_to = [(i, j, lax.rem(zh + d, Z) * 2 + c) for d in range(Z)]
    z_of = [lax.rem(zh + d, Z) for d in range(Z)]
    zsrc = [lax.rem(zh + Z - d, Z) for d in range(Z)]
    partner = (2 * (i // 2) + c, j, 2 * zh + par)
    spread = [(i, lax.rem(j + d, N), 2 * (j // 2) + c) for d in range(N)]
    collect = [(i, 2 * zh + e, 2 * zs + c) for e in range(2) for zs in range(Z)]
    home = j // 2 == zh
    pending = []

    def remote(src, dst, ss, rr, dev):
        return pltpu.make_async_remote_copy(
            src_ref=src, dst_ref=dst, send_sem=ss, recv_sem=rr, device_id=dev, device_id_type=MESH
        )

    def send(src, dst, ss, rr, dev):
        copy = remote(src, dst, ss, rr, dev)
        copy.start()
        pending.append(copy)

    def arrived(dst, ss, rr):
        remote(dst, dst, ss, rr, twin).wait_recv()

    def blk(buf, r, z, first=0, count=TB):
        r = lax.rem(r + 2 * N, N)
        row = pl.multiple_of((r % 2) * TH + z * TB + first, 16)
        return buf.at[r // 2, pl.ds(row, count), :]

    pre_in = pltpu.make_async_copy(pre_ref, pre_own, pre_sem.at[2])
    pre_in.start()

    local = []
    for w_ref, w_v, s in ((wd_ref, wd_v, 0), (wu_ref, wu_v, 1)):
        for m in range(M):
            cols = pl.ds(pl.multiple_of((2 * m + c) * FB, 128), FB)
            cp = pltpu.make_async_copy(w_ref.at[:, cols], w_v.at[m, own_rows, :], loc_sem.at[s, m])
            cp.start()
            local.append(cp)

    barrier = pltpu.get_barrier_semaphore()

    def greet(dev):
        pl.semaphore_signal(barrier, inc=1, device_id=dev, device_id_type=MESH)

    for dev in (twin, y_to[0], y_to[1], z_to[1], z_to[2], z_to[3]):
        greet(dev)

    @pl.when(c != par)
    def _():
        greet(partner)

    for d in range(N):
        if d == 0:
            @pl.when(jnp.logical_not(home))
            def _():
                greet(spread[0])
        else:
            greet(spread[d])
    for dev in collect:
        @pl.when(jnp.logical_not((dev[1] == j) & (dev[2] == a)))
        def _():
            greet(dev)
    swap = jnp.where(c != par, 1, 0)
    both = jnp.where(home, 14, 16)

    pre_in.wait()
    act_own[...] = gelu_parts(pre_own[...].astype(F32).T)[0].astype(BF16)
    pl.semaphore_wait(barrier, 6 + swap + both)

    def spread_start(src_ref, buf, ss, rr):
        row = pl.multiple_of((j % 2) * DB, 64)
        lane = pl.multiple_of(c * TH + zh * TB, TB)
        dst = buf.at[pl.ds(row, DB), pl.ds(lane, TB)]
        slot = (j % 2) * Z + zh

        @pl.when(home)
        def _():
            pltpu.make_async_copy(src_ref, dst, rr.at[slot]).start()

        @pl.when(jnp.logical_not(home))
        def _():
            remote(src_ref, dst, ss.at[0], rr.at[slot], spread[0]).start()

        for d in range(1, N):
            send(src_ref, dst, ss.at[d], rr.at[slot], spread[d])

    def spread_wait(buf, ss, rr, zs):
        for e in range(2):
            lane = pl.multiple_of(c * TH + zs * TB, TB)
            arrived(buf.at[e * DB:(e + 1) * DB, pl.ds(lane, TB)], ss.at[0], rr.at[e * Z + zs])

    def to_twin(buf, s, zs):
        ref = buf.at[:, pl.ds(pl.multiple_of(c * TH + zs * TB, TB), TB)]
        send(ref, ref, tw_ss.at[s, zs], tw_rs.at[s, zs], twin)

    def from_twin(buf, s, zs):
        ref = buf.at[:, pl.ds(pl.multiple_of((1 - c) * TH + zs * TB, TB), TB)]
        arrived(ref, tw_ss.at[s, zs], tw_rs.at[s, zs])

    def spread_end(src_ref, buf, ss, rr):
        @pl.when(jnp.logical_not(home))
        def _():
            remote(src_ref, buf.at[0:DB, 0:TB], ss.at[0], rr.at[0], spread[0]).wait_send()

    spread_start(g_ref, gbuf, g_ss, g_rs)

    there = 2 * (i // 2) + c

    @pl.when(c == par)
    def _():
        pltpu.make_async_copy(act_own, blk(act, i, zh), act_sem.at[1]).start()
        pltpu.make_async_copy(pre_own, pre_v, pre_sem.at[1]).start()

    @pl.when(c != par)
    def _():
        remote(act_own, blk(act, there, zh), act_sem.at[0], act_sem.at[1], partner).start()
        remote(pre_own, pre_v, pre_sem.at[0], pre_sem.at[1], partner).start()

    def weights_to_twin(w_ref, w_v, s):
        for m in range(M):
            cols = pl.ds(pl.multiple_of((2 * m + 1 - c) * FB, 128), FB)
            send(w_ref.at[:, cols], w_v.at[m, own_rows, :], w_ss.at[s, m], w_rs.at[s, m], twin)

    def weights_wait(w_v, s):
        for m in range(M):
            local[s * M + m].wait()
            arrived(w_v.at[m, other_rows, :], w_ss.at[s, m], w_rs.at[s, m])

    weights_to_twin(wd_ref, wd_v, 0)

    class Gather:
        def __init__(self, buf, base, count, rows, sems):
            self.buf, self.base, self.count, self.rows, self.sems = buf, base, count, rows, sems

        def whole(self, r, z):
            return blk(self.buf, r, z, self.base, self.count)

        def first(self, r, z):
            return blk(self.buf, r, z, self.base, self.rows)

        def rest(self, r, z):
            return blk(self.buf, r, z, self.base + self.rows, self.count - self.rows)

        def z_start(self):
            zs, zr = self.sems[:2]
            for d in (2, 1, 3):
                ref = self.whole(i, zh)
                send(ref, ref, zs.at[d], zr.at[d], z_to[d])

        def z_wait(self, d):
            zs, zr = self.sems[:2]
            arrived(self.whole(i, zsrc[d]), zs.at[d], zr.at[d])

        def y_ref(self, r, d):
            return self.first(r, zsrc[d]) if d else self.whole(r, zh)

        def y_send(self, side, s, d):
            ys, yr = self.sems[2:4]
            if s < hops(side, d):
                ref = self.y_ref(i - s if side == 0 else i + s, d)
                send(ref, ref, ys.at[side, s, d], yr.at[side, s, d], y_to[side])

        def y_wait(self, side, s, d):
            ys, yr = self.sems[2:4]
            if s < hops(side, d):
                ref = self.y_ref(i - s - 1 if side == 0 else i + s + 1, d)
                arrived(ref, ys.at[side, s, d], yr.at[side, s, d])

        def b_send(self, side, s):
            if s < hops(side, 0) and self.rows < self.count:
                bs, br = self.sems[4:]
                ref = self.rest(i - s - 1 if side == 0 else i + s + 1, zh)
                for d in (2, 1, 3):
                    send(ref, ref, bs.at[side, s, d], br.at[side, s, d], z_to[d])

        def b_wait(self, s):
            for side in range(2):
                if s < hops(side, 0) and self.rows < self.count:
                    bs, br = self.sems[4:]
                    for d in (1, 3, 2):
                        ref = self.rest(i - s - 1 if side == 0 else i + s + 1, zsrc[d])
                        arrived(ref, bs.at[side, s, d], br.at[side, s, d])

        def step(self, s, ds):
            for d in ds:
                for side in range(2):
                    if s > 0:
                        self.y_wait(side, s - 1, d)
                    self.y_send(side, s, d)

        def low(self, steps):
            for s in steps:
                for side in range(2):
                    self.b_send(side, s)

    far = (1, 3, 2)
    g_act = Gather(act, 0, TB, ACT_ROWS, (a_zs, a_zr, a_ys, a_yr, a_bs, a_br))
    g_hid = [
        Gather(hg, h * HB, HB, HB, (h_zs.at[h], h_zr.at[h], h_ys.at[h], h_yr.at[h])) for h in range(2)
    ]

    arrived(blk(act, i, zh), act_sem.at[0], act_sem.at[1])
    g_act.step(0, (0,))
    arrived(pre_v, pre_sem.at[0], pre_sem.at[1])
    slope[...] = gelu_parts(pre_v[...].astype(F32).T)[1]
    g_act.step(1, (0,))

    def turn(tp, zs):
        lane = pl.multiple_of(tp * TH + zs * TB, TB)
        gt[tp, zs * TB:(zs + 1) * TB, :] = gbuf[:, pl.ds(lane, TB)].T

    for zs in range(Z):
        spread_wait(gbuf, g_ss, g_rs, zs)
        to_twin(gbuf, 0, zs)
        turn(c, zs)
    weights_wait(wd_v, 0)
    def partial(r):
        r = lax.rem(r + 2 * N, N)
        row = pl.multiple_of((r % 2) * TH, TB)
        term = jnp.dot(gt[r % 2], wd_v[r // 2], preferred_element_type=F32)
        p[r // 2, pl.ds(row, TH), :] = term.astype(BF16)

    def rs_out(side, s, d):
        h = hops(side, d)
        return i + h - s if side == 0 else i - h + s

    def rs_at(h, side, s, d):
        return rs.at[side, s, d, h * HB:(h + 1) * HB]

    def p_at(h, r, d):
        return blk(p, r, z_of[d], h * HB, HB)

    def rs_send(h, side, s, d):
        src = p_at(h, rs_out(side, s, d), d) if s == 0 else rs_at(h, side, s - 1, d)
        send(src, rs_at(h, side, s, d), r_ys.at[h, side, s, d], r_yr.at[h, side, s, d], y_to[side])

    def rs_wait(h, side, s, d):
        arrived(rs_at(h, side, s, d), r_ys.at[h, side, s, d], r_yr.at[h, side, s, d])

    def rs_start(h, long):
        for d in Z_ORDER:
            rs_send(h, 0 if (hops(0, d) == 4) == long else 1, 0, d)

    def rs_step(h, s):
        for d in Z_ORDER:
            for side in range(2):
                if s < hops(side, d) - 1:
                    rs_wait(h, side, s, d)
                    mine = p_at(h, rs_out(side, s + 1, d), d)
                    got = rs_at(h, side, s, d)
                    got[...] = (got[...].astype(F32) + mine[...].astype(F32)).astype(BF16)
                    rs_send(h, side, s + 1, d)

    def rs_end(h):
        for d in Z_ORDER:
            total = p_at(h, i, d)[...].astype(F32)
            for side in range(2):
                s = hops(side, d) - 1
                rs_wait(h, side, s, d)
                total = total + rs_at(h, side, s, d)[...].astype(F32)
            if d == 0:
                part[h * HB:(h + 1) * HB] = total
            else:
                out = rs_at(h, 0, hops(0, d) - 1, d)
                out[...] = total.astype(BF16)
                send(out, zrec.at[d, h * HB:(h + 1) * HB], r_zs.at[h, d], r_zr.at[h, d], z_to[d])

    def hidden(h):
        rows = slice(h * HB, (h + 1) * HB)
        total = part[rows]
        for d in far:
            arrived(zrec.at[d, rows], r_zs.at[h, d], r_zr.at[h, d])
            total = total + zrec[d, rows].astype(F32)
        blk(hg, i, zh, h * HB, HB)[...] = (total * slope[rows]).astype(BF16)
        g_hid[h].z_start()
        g_hid[h].step(0, (0,))

    def cross(gather):
        for d in far:
            gather.z_wait(d)
            gather.step(0, (d,))

    def own_tokens(k, carry):
        partial(c + 2 * k)
        return carry
    lax.fori_loop(0, M, own_tokens, 0)

    for zs in range(Z):
        from_twin(gbuf, 0, zs)
        turn(1 - c, zs)

    def pick(mine, other):
        return jnp.where(c == par, mine, other)

    partial(pick(i + 3, i + 4))
    partial(pick(i - 3, i + 2))
    rs_start(0, True)
    rs_start(0, False)
    partial(pick(i + 1, i - 2))
    partial(pick(i - 1, i))
    rs_step(0, 0)
    g_act.step(2, (0,))
    g_act.z_start()
    rs_step(0, 1)
    g_act.low((0, 1))
    g_act.step(3, (0,))
    rs_step(0, 2)
    rs_start(1, True)
    rs_start(1, False)
    weights_to_twin(wu_ref, wu_v, 1)
    g_act.step(4, (0,))
    rs_end(0)
    rs_step(1, 0)
    rs_step(1, 1)
    hidden(0)
    rs_step(1, 2)
    g_hid[0].step(1, (0,))
    cross(g_hid[0])
    rs_end(1)
    g_hid[0].step(2, (0,))
    g_hid[0].step(1, far)
    hidden(1)
    g_hid[0].step(3, (0,))
    g_hid[0].step(2, far)
    g_hid[1].step(1, (0,))
    cross(g_hid[1])
    g_act.low((2, 3))
    spread_start(x_ref, xbuf, x_ss, x_rs)
    g_hid[0].step(3, far)
    g_hid[1].step(2, (0,))
    g_hid[1].step(1, far)
    g_hid[0].step(4, (0,) + far)
    cross(g_act)
    g_hid[1].step(3, (0,))
    g_hid[1].step(2, far)
    g_hid[1].step(3, far)
    g_act.step(1, far)
    weights_wait(wu_v, 1)

    def weight_grad(feat, hid, stage, m):
        term = jnp.dot(feat[...], hid[m], preferred_element_type=F32) * scale
        stage[m] = term.astype(BF16)

    outs = []

    def weight_out(stage, out_ref, s, m):
        cols = pl.ds(pl.multiple_of((2 * m + c) * FB, 128), FB)
        cp = pltpu.make_async_copy(stage.at[m, own_rows, :], out_ref.at[:, cols], loc_sem.at[2 + s, m])
        cp.start()
        outs.append(cp)
        send(stage.at[m, other_rows, :], out_ref.at[:, cols], o_ss.at[s, m], o_rs.at[s, m], twin)

    def weight_arrived(out_ref, s, m):
        cols = pl.ds(pl.multiple_of((2 * m + 1 - c) * FB, 128), FB)
        arrived(out_ref.at[:, cols], o_ss.at[s, m], o_rs.at[s, m])

    early = 1 - par
    last = lax.rem(i + 4, N) // 2

    def input_part(tp, m):
        row = pl.multiple_of(tp * TH, TB)
        return lax.dot_general(
            wu_v[m], hg[m, pl.ds(row, TH), :], (((1,), (1,)), ((), ())),
            preferred_element_type=F32,
        )

    def input_done(tp, zs, total):
        qb[tp, :, zs * TB:(zs + 1) * TB] = total.astype(BF16)

        @pl.when(c != tp)
        def _():
            cols = slice(zs * TB, (zs + 1) * TB)
            remote(qb.at[tp, :, cols], qt.at[:, cols], tw_ss.at[2, zs], tw_rs.at[2, zs], twin).start()

    def input_out(tp):
        @pl.when(c == tp)
        def _():
            for zs in range(Z):
                cols = slice(zs * TB, (zs + 1) * TB)
                arrived(qt.at[:, cols], tw_ss.at[2, zs], tw_rs.at[2, zs])
                qb[c, :, cols] = (qb[c, :, cols].astype(F32) + qt[:, cols].astype(F32)).astype(BF16)
                for e in range(2):
                    dev = collect[e * Z + zs]
                    mine = (dev[1] == j) & (dev[2] == a)
                    src = qb.at[c, e * DB:(e + 1) * DB, cols]

                    @pl.when(mine)
                    def _():
                        pltpu.make_async_copy(src, qrec.at[j], q_rs.at[j]).start()

                    @pl.when(jnp.logical_not(mine))
                    def _():
                        remote(src, qrec.at[j], q_ss.at[e * Z + zs], q_rs.at[j], dev).start()

    qacc[...] = input_part(early, 0)
    for m in range(1, M):
        qacc[...] += input_part(early, m)
    for zs in range(Z):
        input_done(early, zs, qacc[:, zs * TB:(zs + 1) * TB])
    qacc[...] = input_part(par, lax.rem(last + 1, M))
    for m in (2, 3):
        qacc[...] += input_part(par, lax.rem(last + m, M))
    input_out(early)
    for zs in range(Z):
        spread_wait(xbuf, x_ss, x_rs, zs)
        to_twin(xbuf, 1, zs)
    g_hid[1].step(4, (0,) + far)
    for zs in range(Z):
        row = pl.multiple_of(par * TH + zs * TB, TB)
        term = lax.dot_general(
            wu_v[last], hg[last, pl.ds(row, TB), :], (((1,), (1,)), ((), ())),
            preferred_element_type=F32,
        )
        input_done(par, zs, qacc[:, zs * TB:(zs + 1) * TB] + term)
    g_act.step(2, far)
    input_out(par)
    for zs in range(Z):
        from_twin(xbuf, 1, zs)
    for m in (1, 2, 3):
        weight_grad(xbuf, hg, stage_u, lax.rem(last + m, M))
        weight_out(stage_u, du_ref, 1, lax.rem(last + m, M))
    weight_grad(xbuf, hg, stage_u, last)
    weight_out(stage_u, du_ref, 1, last)
    g_act.step(3, far)
    for step in range(4):
        g_act.b_wait(step)
    for m in (1, 2, 3):
        weight_grad(gbuf, act, stage_d, lax.rem(last + m, M))
        weight_out(stage_d, dd_ref, 0, lax.rem(last + m, M))
    g_act.step(4, far)
    weight_grad(gbuf, act, stage_d, last)
    weight_out(stage_d, dd_ref, 0, last)

    total = jnp.zeros((DB, TB), F32)
    for d in range(N):
        arrived(qrec.at[d], q_ss.at[0], q_rs.at[d])
        total = total + qrec[d].astype(F32)
    ig_ref[...] = total.astype(BF16)

    for s, out_ref in ((0, dd_ref), (1, du_ref)):
        for m in range(M):
            weight_arrived(out_ref, s, m)
    for cp in outs:
        cp.wait()
    for copy in pending:
        copy.wait_send()
    spread_end(g_ref, gbuf, g_ss, g_rs)
    spread_end(x_ref, xbuf, x_ss, x_rs)

    @pl.when(c != par)
    def _():
        remote(act_own, blk(act, there, zh), act_sem.at[0], act_sem.at[1], partner).wait_send()
        remote(pre_own, pre_v, pre_sem.at[0], pre_sem.at[1], partner).wait_send()

    for zs in range(Z):
        cols = slice(zs * TB, (zs + 1) * TB)
        remote(qb.at[0, :, cols], qt.at[:, cols], tw_ss.at[2, zs], tw_rs.at[2, zs], twin).wait_send()
    for e in range(2):
        for zs in range(Z):
            dev = collect[e * Z + zs]
            src = qb.at[c, e * DB:(e + 1) * DB, zs * TB:(zs + 1) * TB]

            @pl.when(jnp.logical_not((dev[1] == j) & (dev[2] == a)))
            def _():
                remote(src, qrec.at[j], q_ss.at[e * Z + zs], q_rs.at[j], dev).wait_send()


def hand_over(ig_in, du_in, dd_in, ig_out, du_out, dd_out, ig_v, du_v, dd_v, in_sem, out_sem):
    parts = [(ig_in, ig_v, ig_out)]
    for src, mid, dst in ((du_in, du_v, du_out), (dd_in, dd_v, dd_out)):
        for part in range(4):
            rows = pl.ds(part * (DB // 4), DB // 4)
            parts.append((src.at[rows, :], mid.at[rows, :], dst.at[rows, :]))
    loads = [pltpu.make_async_copy(src, mid, in_sem.at[n]) for n, (src, mid, _) in enumerate(parts)]
    stores = [pltpu.make_async_copy(mid, dst, out_sem.at[n]) for n, (_, mid, dst) in enumerate(parts)]
    for load in loads:
        load.start()
    for load, store in zip(loads, stores):
        load.wait()
        store.start()
    for store in stores:
        store.wait()


def shards(inputs, out_grad, pre_act, w_up, w_down):
    scale = float(inputs.shape[1] * N) ** (-0.5)
    dma = pltpu.SemaphoreType.DMA
    any_spec = pl.BlockSpec(memory_space=pl.ANY)
    results = pl.pallas_call(
        functools.partial(kernel, scale),
        out_shape=(
            jax.ShapeDtypeStruct((DB, TB), BF16),
            jax.ShapeDtypeStruct((DB, N * FB), BF16),
            jax.ShapeDtypeStruct((DB, N * FB), BF16),
        ),
        in_specs=[any_spec] * 5,
        out_specs=(pl.BlockSpec(memory_space=pltpu.VMEM), any_spec, any_spec),
        scratch_shapes=[
            pltpu.VMEM((DC, 2 * TH), BF16),
            pltpu.VMEM((DC, 2 * TH), BF16),
            pltpu.VMEM((2, TH, DC), BF16),
            pltpu.VMEM((M, DC, FB), BF16),
            pltpu.VMEM((M, DC, FB), BF16),
            pltpu.VMEM((M, 2 * TH, FB), BF16),
            pltpu.VMEM((2, 4, Z, TB, FB), BF16),
            pltpu.VMEM((Z, TB, FB), BF16),
            pltpu.VMEM((M, 2 * TH, FB), BF16),
            pltpu.VMEM((M, 2 * TH, FB), BF16),
            pltpu.VMEM((FB, TB), BF16),
            pltpu.VMEM((TB, FB), F32),
            pltpu.VMEM((TB, FB), F32),
            pltpu.VMEM((M, DC, FB), BF16),
            pltpu.VMEM((M, DC, FB), BF16),
            pltpu.VMEM((2, DC, TH), BF16),
            pltpu.VMEM((DC, TH), BF16),
            pltpu.VMEM((N, DB, TB), BF16),
            pltpu.VMEM((FB, TB), BF16),
            pltpu.VMEM((TB, FB), BF16),
            pltpu.VMEM((DC, TH), F32),
            dma((4, M)), dma((3,)), dma((2,)), dma((2, 4, Z)), dma((2, 4, Z)),
             dma((N,)), dma((N,)), dma((N,)), dma((N,)),
            dma((3, Z)), dma((3, Z)), dma((2, M)), dma((2, M)),
            dma((Z,)), dma((Z,)), dma((2, 4, Z)), dma((2, 4, Z)),
            dma((2, Z)), dma((2, Z)), dma((2, 2, 4, Z)), dma((2, 2, 4, Z)),
            dma((2, Z)), dma((2, Z)), dma((2, 2, 4, Z)), dma((2, 2, 4, Z)),
            dma((2, M)), dma((2, M)), dma((N,)), dma((N,)),
        ],
        compiler_params=pltpu.CompilerParams(
            collective_id=0, has_side_effects=True, vmem_limit_bytes=60 * 2**20
        ),
    )(inputs, out_grad, pre_act, w_up, w_down)
    return pl.pallas_call(
        hand_over,
        out_shape=[jax.ShapeDtypeStruct(value.shape, value.dtype) for value in results],
        in_specs=[any_spec] * 3,
        out_specs=[any_spec] * 3,
        scratch_shapes=[pltpu.VMEM(value.shape, value.dtype) for value in results] + [dma((9,)), dma((9,))],
        compiler_params=pltpu.CompilerParams(vmem_limit_bytes=60 * 2**20),
    )(*results)


def solution(mesh):
    in_specs = (
        P(("ia", "ja"), "al"),
        P(("ia", "ja"), "al"),
        P(("ja", "ia"), "al"),
        P(("ia", "al"), "ja"),
        P(("ia", "al"), "ja"),
    )
    out_specs = (P(("ia", "ja"), "al"), P(("ia", "al"), "ja"), P(("ia", "al"), "ja"))
    return jax.shard_map(shards, mesh=mesh, in_specs=in_specs, out_specs=out_specs, check_vma=False)
```
